128 devices in a mesh: section: 2 (over core), row: 4 (over y), col: 16 (over x, z).
Axes of the slice: x: 4, y: 4, z: 4, core: 2. Of those that a mesh axis runs over, the one named last changes fastest.
Arguments:
- images: bfloat16 [2, 128, 50, 768], P(None, ('row', 'col')), may hold values from -6 to 6
- cotangent: bfloat16 [2, 128, 50, 768], P(None, ('row', 'col')), may hold values from -6 to 6
- norm_gains: bfloat16 [2, 2, 768], P('section', None, ('row', 'col')), may hold values from 0.25 to 1.75
- attn_qkv: bfloat16 [2, 768, 3, 768], P('section', 'col', None, 'row'), may hold values from -0.21875 to 0.21875
- attn_out: bfloat16 [2, 768, 768], P('section', 'row', 'col'), may hold values from -0.875 to 0.875
- router: bfloat16 [2, 768, 32], P('section', ('row', 'col')), may hold values from -0.15625 to 0.15625
- expert_in: bfloat16 [2, 768, 98304], P('section', None, ('row', 'col')), may hold values from -0.21875 to 0.21875
- expert_out: bfloat16 [2, 98304, 768], P('section', ('row', 'col')), may hold values from -1.75 to 1.75
- routes: int32 [2, 2, 128, 50, 2], P('section', None, ('row', 'col')), may hold values from 0 to 31, all different within a row; in each aligned block of 100 rows (0 to 99, 100 to 199, ..., all dimensions but the last counted through in order) at most 8 rows name the same one
Outputs:
- section_out: bfloat16 [2, 2, 128, 50, 768], P('section', None, ('row', 'col'))
- input_grads: float32 [2, 2, 128, 50, 768], P('section', None, ('row', 'col'))
- grad_gains: float32 [2, 2, 768], P('section', None, ('row', 'col'))
- grad_qkv: float32 [2, 768, 3, 768], P('section', 'col', None, 'row')
- grad_attn_out: float32 [2, 768, 768], P('section', 'row', 'col')
- grad_router: float32 [2, 768, 32], P('section', ('row', 'col'))
- grad_expert_in: float32 [2, 768, 98304], P('section', None, ('row', 'col'))
- grad_expert_out: float32 [2, 98304, 768], P('section', ('row', 'col'))
The draws below stay inside these ranges and needn't reach their ends.
Inputs may be any that keep to these rules, and one draw needn't show every extreme that they name: `routes`: each token names two different experts; among the tokens of one device of one section and micro-batch (aligned blocks of 100 tokens) no expert is named more than 8 times, a bound that some block reaches.
All inputs are finite; a program needn't handle non-finite values.
Results may differ from the reference program's by a relative error of at most 0.03.
Values may be sent and summed in bfloat16 or wider, within the bound.
No kernel may reach another device: no remote copies, remote signals or barrier semaphores. Data moves between devices by JAX's collectives and lax.ppermute only.
A program may use at most 192 MiB of HBM per device.

```python
import math
import jax
import jax.numpy as jnp
import numpy as np
from jax import lax

D = 768
HEADS = 12
HEAD = 64
FF = 3072
SEQ = 50
IMG_DEV = 2
MICRO = 2
SECTIONS = 2
EXPERTS = 32
IMAGES = 128
CAP = 8
N_ROW = 4
N_COL = 16


def levels(key, extent, shards, smallest, top_value):
    factor_of = 1.0
    for axis_at, shards_of in shards:
        draws = jax.random.uniform(jax.random.fold_in(jax.random.fold_in(key, 6), axis_at), (shards_of,), jnp.float32, smallest / len(shards), top_value / len(shards))
        factor_of = factor_of * jnp.repeat(jnp.exp(draws), extent[axis_at] // shards_of).reshape((-1,) + (1,) * (len(extent) - 1 - axis_at))
    return factor_of


def routed_block(own_key, own, number, rows, count, top, most, slope):
    sequence = jax.random.permutation(own_key, count)
    packed, common = shares(count, rows * top, most, slope, True), shares(count, rows * top, most, slope, False)
    places = jnp.arange(count)

    def named(sizes, offset_by):
        used = int((sizes > 0).sum())
        fixed = max(1, used // 4)
        moved = fixed + (places - fixed + offset_by * (used - fixed)) % max(1, count - fixed)
        return jnp.zeros((count,), jnp.int32).at[sequence[jnp.where(places < fixed, places, moved)]].set(jnp.asarray(sizes, jnp.int32))

    sizes = jnp.where(number % 4 == 0, named(packed, number // 4), named(common, number - number // 4 - 1))
    mixed = jax.random.permutation(jax.random.fold_in(own, 3), count)
    source_of, receiver = mixed[0:count // 2 * 2:2], mixed[1:count // 2 * 2:2]
    margin = jnp.minimum(sizes[source_of] - 1, most - sizes[receiver]) // 2
    margin = jnp.where((source_of == sequence[0]) | (receiver == sequence[0]) | (sizes[receiver] == 0), 0, jnp.maximum(margin, 0))
    moved = jax.random.randint(jax.random.fold_in(own, 4), (count // 2,), 0, 1 << 20) % (margin + 1)
    sizes = sizes.at[source_of].add(-moved).at[receiver].add(moved)
    items = jnp.searchsorted(jnp.cumsum(sizes), jnp.arange(rows * top), side="right").astype(jnp.int32)
    listing = items.reshape(top, rows).T
    listing = listing[jax.random.permutation(jax.random.fold_in(own, 1), rows)]
    offset_by = jax.random.randint(jax.random.fold_in(own, 2), (rows, 1), 0, top)
    return jnp.take_along_axis(listing, (jnp.arange(top)[None, :] + offset_by) % top, axis=1)


def shares(number_of, total, most, lean, full):
    weights = [(1 << 20) // math.isqrt(grade ** lean) + 1 for grade in range(1, number_of + 1)]
    largest = most if full else min(most, max(-(-total // number_of), total * weights[0] // sum(weights)))
    least = 1 if total - largest >= number_of - 1 else 0
    given, rest = [largest] + [least] * (number_of - 1), total - largest - least * (number_of - 1)
    while rest > 0:
        free = [i for i in range(1, number_of) if given[i] < largest] or [i for i in range(1, number_of) if given[i] < most]
        mass, budget = sum([weights[i] for i in free]), rest
        for i in free:
            addition = min(most - given[i], max(1, budget * weights[i] // mass), rest)
            given[i] = given[i] + addition
            rest = rest - addition
    return np.array(given)


def scatter_about(key, dims, deviation, most, cuts=(), kind=jnp.bfloat16):
    result = jax.random.normal(key, dims, jnp.float32) * deviation
    if len(cuts) > 0:
        result = levels(key, dims, cuts, -0.22, 0.18) * result
    return jnp.clip(result, min=-most, max=most).astype(kind)


def setup_inputs(seed: int = 0) -> dict:
    seeds = jax.random.split(jax.random.key(seed), 10)
    images = scatter_about(seeds[0], (MICRO, IMAGES, SEQ, D), 1.0, 6.0, ((1, 64),))
    cotangent = scatter_about(seeds[1], (MICRO, IMAGES, SEQ, D), 1.0, 6.0, ((1, 64),))
    norm_gains = jnp.clip(1.0 + 0.15 * jax.random.normal(seeds[2], (SECTIONS, 2, D), jnp.float32), 0.25, 1.75).astype(jnp.bfloat16)
    attn_qkv = scatter_about(seeds[3], (SECTIONS, D, 3, D), D ** -0.5, 0.21875, ((0, 2), (1, 16), (3, 4)))
    attn_out = scatter_about(seeds[4], (SECTIONS, D, D), (D // 16) ** -0.5, 0.875, ((0, 2), (1, 4), (2, 16)))
    router = scatter_about(seeds[5], (SECTIONS, D, EXPERTS), (2 * D) ** -0.5, 0.15625, ((0, 2), (1, 64)))
    expert_in = scatter_about(seeds[6], (SECTIONS, D, EXPERTS * FF), D ** -0.5, 0.21875, ((0, 2), (2, 64)))
    expert_out = scatter_about(seeds[7], (SECTIONS, EXPERTS * FF, D), (max(FF // 256, 1)) ** -0.5, 1.75, ((0, 2), (1, 64)))
    routes_keys = jax.random.split(jax.random.fold_in(seeds[8], 1), SECTIONS * MICRO * IMAGES * SEQ // (IMG_DEV * SEQ))
    routes_turns = jax.random.permutation(jax.random.fold_in(seeds[8], 3), SECTIONS * MICRO * IMAGES * SEQ // (IMG_DEV * SEQ))
    routes = jax.vmap(lambda own, number: routed_block(jax.random.fold_in(seeds[8], 2), own, number, IMG_DEV * SEQ, EXPERTS, 2, CAP, 1))(routes_keys, routes_turns).reshape((SECTIONS, MICRO, IMAGES, SEQ, 2))
    return dict(images=images, cotangent=cotangent, norm_gains=norm_gains, attn_qkv=attn_qkv, attn_out=attn_out, router=router, expert_in=expert_in, expert_out=expert_out, routes=routes)


@jax.custom_vjp
def low(v):
    return lax.optimization_barrier(v.astype(jnp.bfloat16)).astype(jnp.float32)

@jax.custom_vjp
def low_back(v):
    return v

def low_keep(v):
    return (low(v), None)

def low_pass(kept, grad):
    return (grad,)

def back_keep(v):
    return (v, None)

def back_low(kept, grad):
    return (low(grad),)
low.defvjp(low_keep, low_pass)
low_back.defvjp(back_keep, back_low)
epsilon = 1e-06
highest = lax.Precision.HIGHEST

def layer_norm(values, gain_row):
    centred = values - lax.optimization_barrier(jnp.mean(values, axis=-1, keepdims=True))
    spread = lax.optimization_barrier(jnp.mean(centred * centred, axis=-1, keepdims=True))
    return centred * lax.rsqrt(spread + epsilon) * gain_row

def positions(chosen_ids):
    devices = N_ROW * N_COL
    flat_ids = chosen_ids.reshape(MICRO, devices, IMG_DEV * SEQ * 2).astype(jnp.int32)
    one_hot = (flat_ids[..., None] == jnp.arange(EXPERTS, dtype=jnp.int32)).astype(jnp.int32)
    earlier = jnp.cumsum(one_hot, axis=2) - one_hot
    slot_ids = lax.optimization_barrier(jnp.sum(earlier * one_hot, axis=3))
    sources = jnp.arange(devices, dtype=jnp.int32)[None, :, None]
    spots = flat_ids * (devices * CAP) + sources * CAP + slot_ids
    return spots.reshape(MICRO, devices * IMG_DEV * SEQ * 2)

def run_expert(pack):
    block_rows, first_one, second_one = pack
    half_width = FF // 2
    rows_in = low_back(block_rows)
    total = jnp.zeros(block_rows.shape, jnp.float32)
    for half_id in range(2):
        start = half_id * half_width
        first_half = first_one[:, start:start + half_width]
        second_half = second_one[start:start + half_width]
        preact = low_back(jnp.dot(rows_in, first_half, precision=highest))
        activated = low(jax.nn.gelu(preact, approximate=False))
        total = total + jnp.dot(activated, second_half, precision=highest)
    return low(low_back(total))

def moe_layer(section_in, gains, qkv_w, out_w, router_w, first_w, second_w, chosen_ids, spots):
    normed = low(layer_norm(section_in, gains[0]))
    mixed = low(low_back(jnp.einsum('misd,dke->miske', normed, qkv_w, precision=highest)))
    split_heads = mixed.reshape(MICRO, IMAGES, SEQ, 3, HEADS, HEAD)
    query = split_heads[:, :, :, 0]
    key_part = split_heads[:, :, :, 1]
    value_part = split_heads[:, :, :, 2]
    scores = low_back(jnp.einsum('mishd,mithd->mihst', query, key_part, precision=highest) * HEAD ** (-0.5))
    weights = low(jax.nn.softmax(scores, axis=-1))
    attended = jnp.einsum('mihst,mithd->mishd', weights, value_part, precision=highest)
    attended = low(low_back(attended.reshape(MICRO, IMAGES, SEQ, D)))
    branch = low_back(jnp.einsum('misd,de->mise', attended, out_w, precision=highest))
    hidden = section_in + branch
    normed_two = low(layer_norm(hidden, gains[1]))
    token_rows = normed_two.reshape(MICRO, IMAGES * SEQ, D)
    logits = low_back(jnp.einsum('mnd,de->mne', token_rows, router_w, precision=highest))
    chance = jax.nn.softmax(logits, axis=-1)
    route_ids = chosen_ids.reshape(MICRO, IMAGES * SEQ, 2).astype(jnp.int32)
    gate_values = jnp.take_along_axis(chance, route_ids, axis=2)
    repeated = jnp.repeat(token_rows, 2, axis=1)
    slots_all = N_ROW * N_COL * CAP

    def fill(spot_row, rows_in):
        return jnp.zeros((EXPERTS * slots_all, D), jnp.float32).at[spot_row].set(rows_in)
    buffers = jax.vmap(fill)(spots, repeated)
    buffers = buffers.reshape(MICRO, EXPERTS, slots_all, D).transpose(1, 0, 2, 3).reshape(EXPERTS, MICRO * slots_all, D)
    first_all = first_w.reshape(D, EXPERTS, FF).transpose(1, 0, 2)
    second_all = second_w.reshape(EXPERTS, FF, D)
    results = lax.map(jax.checkpoint(run_expert), (buffers, first_all, second_all))
    results = results.reshape(EXPERTS, MICRO, slots_all, D).transpose(1, 0, 2, 3).reshape(MICRO, EXPERTS * slots_all, D)

    def pick(table_rows, spot_row):
        return jnp.take(table_rows, spot_row, axis=0)
    picked = jax.vmap(pick)(results, spots).reshape(MICRO, IMAGES * SEQ, 2, D)
    mixture = lax.optimization_barrier(jnp.sum(gate_values[..., None] * picked, axis=2))
    return hidden + mixture.reshape(MICRO, IMAGES, SEQ, D)

def reference(images, cotangent, norm_gains, attn_qkv, attn_out, router, expert_in, expert_out, routes):
    spot_list = [positions(routes[section_id]) for section_id in range(2)]

    def forward(first_in, probe, gains, qkv_w, out_w, router_w, first_w, second_w):
        middle = low(low_back(moe_layer(first_in, gains[0], qkv_w[0], out_w[0], router_w[0], first_w[0], second_w[0], routes[0], spot_list[0])))
        final = low(low_back(moe_layer(middle + probe, gains[1], qkv_w[1], out_w[1], router_w[1], first_w[1], second_w[1], routes[1], spot_list[1])))
        return (middle, final)
    floats = (images.astype(jnp.float32), jnp.zeros(images.shape, jnp.float32), norm_gains.astype(jnp.float32), attn_qkv.astype(jnp.float32), attn_out.astype(jnp.float32), router.astype(jnp.float32), expert_in.astype(jnp.float32), expert_out.astype(jnp.float32))
    outputs, pull = jax.vjp(forward, *floats)
    middle, final = outputs
    grads = pull((jnp.zeros_like(middle), cotangent.astype(jnp.float32)))
    section_out = jnp.stack([middle, final]).astype(jnp.bfloat16)
    input_grads = jnp.stack([grads[0], grads[1]])
    return (section_out, input_grads, grads[2], grads[3], grads[4], grads[5], grads[6], grads[7])
```

```python
import functools

import jax
import jax.numpy as jnp
from jax import lax
from jax.experimental import pallas as pl
from jax.experimental.pallas import tpu as pltpu
from jax.sharding import PartitionSpec as P

HEAD = 64
WIDTH = 768
TOKENS = 100
SEQ = 50
PAD = 112
EXPERTS = 32
SLOTS = 8
ROWS = 4
COLS = 16
CHIPS = ROWS * COLS
PART = WIDTH // COLS
SMALL = WIDTH // CHIPS
FILL = CHIPS * SLOTS
HIDDEN = 1536
STEP = 256
EPSILON = 1e-06
SCALE = float(HEAD) ** (-0.5)
VMEM = 58 * 1024 * 1024
BF = jnp.bfloat16
F32 = jnp.float32


def dot(left, right):
    return jnp.dot(left, right, preferred_element_type=F32)


def dot_tn(left, right):
    return lax.dot_general(left, right, (((0,), (0,)), ((), ())), preferred_element_type=F32)


def dot_nt(left, right):
    return lax.dot_general(left, right, (((1,), (1,)), ((), ())), preferred_element_type=F32)


def iota(shape, axis):
    return lax.broadcasted_iota(jnp.int32, shape, axis)


def hot(flag):
    return jnp.where(flag, 1.0, 0.0)


def normalise(values):
    centred = values - jnp.mean(values, axis=-1, keepdims=True)
    spread = jnp.mean(centred * centred, axis=-1, keepdims=True)
    inverse = lax.rsqrt(spread + EPSILON)
    return centred * inverse, inverse


def normalise_back(grad, unit, inverse):
    return inverse * (
        grad
        - jnp.mean(grad, axis=-1, keepdims=True)
        - unit * jnp.mean(grad * unit, axis=-1, keepdims=True)
    )


def gelu_parts(values):
    bell = jnp.exp(-0.5 * values * values)
    t = 1.0 / (1.0 + (0.3275911 * 0.7071067811865476) * jnp.abs(values))
    poly = 1.061405429 * t - 1.453152027
    poly = poly * t + 1.421413741
    poly = poly * t - 0.284496736
    poly = poly * t + 0.254829592
    tail = (0.5 * t) * poly * bell
    below = jnp.where(values < 0, tail, 1.0 - tail)
    return values * below, below + values * (0.3989422804014327 * bell)


def half_turn(values):
    return pltpu.roll(values, HEAD, 1)


def lane_low(rows):
    return iota((rows, 2 * HEAD), 1) < HEAD


def unpack_weights(core, own_ref, other_ref, w_ref):
    def put(from_ref, half):
        for r in range(ROWS):
            for b in range(3):
                at = (3 * half + b) * 128
                block = from_ref[r * COLS : (r + 1) * COLS, b * PART : (b + 1) * PART, :]
                w_ref[r, :, at : at + 128] = block.reshape(WIDTH, 128)

    @pl.when(core == 0)
    def _():
        put(own_ref, 0)
        put(other_ref, 1)

    @pl.when(core == 1)
    def _():
        put(own_ref, 1)
        put(other_ref, 0)


def small_places():
    inside = iota((WIDTH, CHIPS * 16), 1)
    group = lax.shift_right_logical(inside, 4)
    place = jnp.bitwise_and(inside, 15)
    wanted = group * SMALL + place
    return hot((iota((WIDTH, CHIPS * 16), 0) == wanted) & (place < SMALL)).astype(BF)


def unpack_small(own_ref):
    packed = own_ref[:, 3 * PART : 3 * PART + 16, :].reshape(CHIPS * 16, 128)
    small = dot(small_places(), packed).astype(BF)
    pick = hot(iota((8, 128), 1) == iota((8, 128), 0) + EXPERTS).astype(BF)
    gains = dot_nt(pick, small)
    return small, gains[0:1], gains[1:2]


def routing(route_ref):
    first = route_ref[:, 0:1]
    second = route_ref[:, 1:2]
    lane = iota((PAD, 128), 1)
    hot0 = hot(lane == first)
    hot1 = hot(lane == second)
    before = hot(iota((PAD, PAD), 0) > iota((PAD, PAD), 1)).astype(BF)
    earlier = dot(before, (hot0 + hot1).astype(BF))
    place = iota((PAD, FILL), 1)

    def spread(expert, marks):
        slot = jnp.sum(earlier * marks, axis=1, keepdims=True).astype(jnp.int32)
        base = expert * (2 * SLOTS) + slot
        return hot((place == base) | (place == base + SLOTS)).astype(BF)

    return hot0, hot1, spread(first, hot0), spread(second, hot1)


def gates(chance, marks):
    return jnp.sum(chance * marks, axis=1, keepdims=True)


def image_bias():
    def image(axis):
        at = iota((PAD, PAD), axis)
        return (at >= SEQ).astype(jnp.int32) + (at >= 2 * SEQ).astype(jnp.int32)

    bias = jnp.where(image(0) == image(1), 0.0, -1e30)
    return jnp.concatenate([bias] * 3, axis=0)


def attention_forward(x, w_ref, gain, m_ref, p_ref, o_ref):
    unit, _ = normalise(x)
    a = (unit * gain).astype(BF)
    low = lane_low(PAD)
    low_b = hot(low).astype(BF)
    high_b = (1.0 - hot(low)).astype(BF)
    bias = image_bias()
    branch = jnp.zeros((PAD, WIDTH), F32)
    for r in range(ROWS):
        wide = dot(a, w_ref[r, :, 0:512])
        m5 = dot(a, w_ref[r, :, 640:768]).astype(BF)
        m = wide.astype(BF)
        m_ref[:, r * 640 : r * 640 + 512] = m
        m_ref[:, r * 640 + 512 : r * 640 + 640] = m5
        q, k, v, qk = m[:, 0:128], m[:, 128:256], m[:, 256:384], m[:, 384:512]
        k2 = half_turn(wide[:, 384:512]).astype(BF)
        qs = jnp.concatenate([q * low_b, q * high_b], axis=0)
        s = jnp.concatenate([dot_nt(qs, k), dot_nt(qk * low_b, k2)], axis=0)
        s = s * SCALE + bias
        e = jnp.exp(s - jnp.max(s, axis=-1, keepdims=True))
        p = (e / jnp.sum(e, axis=-1, keepdims=True)).astype(BF)
        p_ref[r * 3 * PAD : (r + 1) * 3 * PAD, :] = p
        os = dot(p[: 2 * PAD], v)
        o2 = dot(p[2 * PAD :], m5)
        o01 = jnp.where(low, os[:PAD], os[PAD:])
        o2 = jnp.where(low, 0.0, half_turn(o2))
        o = jnp.concatenate([o01, o2], axis=1).astype(BF)
        o_ref[:, r * 256 : (r + 1) * 256] = o
        branch = branch + dot_nt(o, w_ref[r, :, 512:768])
    return x + branch


def route_forward(h, small, gain):
    unit, _ = normalise(h)
    b = (unit * gain).astype(BF)
    logits = dot(b, small)
    inside = iota((PAD, 128), 1) < EXPERTS
    logits = jnp.where(inside, logits, -1e30)
    e = jnp.exp(logits - jnp.max(logits, axis=-1, keepdims=True))
    e = jnp.where(inside, e, 0.0)
    return b, e / jnp.sum(e, axis=-1, keepdims=True)


def attention_backward(dh, x, gain, w_ref, m_ref, p_ref, o_ref, g_ref):
    db = dh.astype(BF)
    unit, inverse = normalise(x)
    a = (unit * gain).astype(BF)
    low = lane_low(PAD)
    low_b = hot(low).astype(BF)
    high_b = (1.0 - hot(low)).astype(BF)
    da = jnp.zeros((PAD, WIDTH), F32)
    for r in range(ROWS):
        o = o_ref[:, r * 256 : (r + 1) * 256]
        q = m_ref[:, r * 640 : r * 640 + 128]
        k = m_ref[:, r * 640 + 128 : r * 640 + 256]
        v = m_ref[:, r * 640 + 256 : r * 640 + 384]
        qk = m_ref[:, r * 640 + 384 : r * 640 + 512]
        m5 = m_ref[:, r * 640 + 512 : r * 640 + 640]
        k2 = half_turn(qk.astype(F32)).astype(BF)
        q2 = qk * low_b
        qs = jnp.concatenate([q * low_b, q * high_b], axis=0)
        pb = p_ref[r * 3 * PAD : (r + 1) * 3 * PAD, :]
        p = pb.astype(F32)
        do = dot(db, w_ref[r, :, 512:768])
        do01 = do[:, 0:128].astype(BF)
        do2 = half_turn(do[:, 128:256]).astype(BF) * low_b
        dos = jnp.concatenate([do01 * low_b, do01 * high_b], axis=0)
        dp = jnp.concatenate([dot_nt(dos, v), dot_nt(do2, m5)], axis=0)
        ds = (p * (dp - jnp.sum(dp * p, axis=-1, keepdims=True))).astype(BF)
        dv = dot_tn(pb[: 2 * PAD], dos)
        dv2 = dot_tn(pb[2 * PAD :], do2)
        dqs = dot(ds[: 2 * PAD], k)
        dq = jnp.where(low, dqs[:PAD], dqs[PAD:]) * SCALE
        dk = dot_tn(ds[: 2 * PAD], qs) * SCALE
        dq2 = dot(ds[2 * PAD :], k2) * SCALE
        dk2 = dot_tn(ds[2 * PAD :], q2) * SCALE
        dqk = jnp.where(low, dq2, half_turn(dk2))
        dm = jnp.concatenate([dq, dk, dv, dqk, dv2], axis=1).astype(BF)
        da = da + dot_nt(dm[:, :512], w_ref[r, :, 0:512]) + dot_nt(dm[:, 512:], w_ref[r, :, 640:768])
        gm = dot_tn(a, dm)
        go = dot_tn(db, o)
        blocks = [gm[:, i * 128 : (i + 1) * 128] for i in range(4)]
        blocks += [go[:, :128], gm[:, 512:640] + go[:, 128:256]]
        for i, block in enumerate(blocks):
            g_ref[r * COLS : (r + 1) * COLS, i * PART : (i + 1) * PART, :] = block.astype(BF).reshape(
                COLS, PART, 128
            )
    dx = dh + normalise_back(da * gain, unit, inverse)
    return dx, (da * unit).astype(BF)


def layer_backward(dz, dr, marks, dgv, x, h, b, chance, small, gain1, gain2, w_ref, m_ref, p_ref, o_ref, g_ref):
    _, _, d0, d1 = marks
    dn = dot(d0, dr).astype(BF).astype(F32) + dot(d1, dr).astype(BF).astype(F32)
    dl = (chance * (dgv - jnp.sum(dgv * chance, axis=1, keepdims=True))).astype(BF)
    dn = dn + dot_nt(dl, small)
    unit, inverse = normalise(h)
    dh = dz + normalise_back(dn * gain2, unit, inverse)
    dx, terms = attention_backward(dh, x, gain1, w_ref, m_ref, p_ref, o_ref, g_ref)
    lane = iota((PAD, 128), 1)
    gs = dot_tn(b, dl)
    gs = gs + dot_tn(terms, hot(lane == EXPERTS).astype(BF))
    gs = gs + dot_tn((dn * unit).astype(BF), hot(lane == EXPERTS + 1).astype(BF))
    spread = dot_tn(small_places(), gs.astype(BF)).astype(BF)
    g_ref[:, 6 * PART : 6 * PART + 16, :] = spread.reshape(CHIPS, 16, 128)
    return dx


def gate_grads(dz, y_both, marks):
    hot0, hot1 = marks[0], marks[1]
    dg0 = jnp.sum(dz * y_both[:, :WIDTH].astype(F32), axis=1, keepdims=True)
    dg1 = jnp.sum(dz * y_both[:, WIDTH:].astype(F32), axis=1, keepdims=True)
    return dg0 * hot0 + dg1 * hot1


def grad_rows(dz, chance, marks):
    hot0, hot1, d0, d1 = marks
    dy0 = (gates(chance, hot0) * dz).astype(BF)
    dy1 = (gates(chance, hot1) * dz).astype(BF)
    return (dot_tn(d0, dy0) + dot_tn(d1, dy1)).astype(BF)


def combine(h, returned, chance, marks):
    hot0, hot1, d0, d1 = marks
    y0 = dot(d0, returned).astype(BF)
    y1 = dot(d1, returned).astype(BF)
    z = h + gates(chance, hot0) * y0.astype(F32) + gates(chance, hot1) * y1.astype(F32)
    return z, jnp.concatenate([y0, y1], axis=1)


def first_kernel(core_ref, x_ref, route_ref, own_ref, other_ref, buf_ref, m_ref, p_ref, o_ref, h_ref, b_ref, c_ref, w_ref):
    unpack_weights(core_ref[0], own_ref, other_ref, w_ref)
    small, gain1, gain2 = unpack_small(own_ref)
    marks = routing(route_ref)
    h = attention_forward(x_ref[...].astype(F32), w_ref, gain1, m_ref, p_ref, o_ref)
    b, chance = route_forward(h, small, gain2)
    h_ref[...] = h
    b_ref[...] = b
    c_ref[...] = chance
    buf_ref[...] = dot_tn(marks[2] + marks[3], b).astype(BF)


def middle_kernel(core_ref, back_ref, h0_ref, c0_ref, route0_ref, route1_ref, cot_ref, own_ref, other_ref, x_ref, y_ref, buf_ref, m_ref, p_ref, o_ref, h_ref, b_ref, c_ref, w_ref):
    unpack_weights(core_ref[0], own_ref, other_ref, w_ref)
    z, y_both = combine(h0_ref[...], back_ref[...], c0_ref[...], routing(route0_ref))
    x = z.astype(BF)
    x_ref[...] = x
    y_ref[...] = y_both
    small, gain1, gain2 = unpack_small(own_ref)
    marks = routing(route1_ref)
    h = attention_forward(x.astype(F32), w_ref, gain1, m_ref, p_ref, o_ref)
    b, chance = route_forward(h, small, gain2)
    h_ref[...] = h
    b_ref[...] = b
    c_ref[...] = chance
    buf_ref[:, :WIDTH] = dot_tn(marks[2] + marks[3], b).astype(BF)
    buf_ref[:, WIDTH:] = grad_rows(cot_ref[...].astype(F32), chance, marks)


def turn_kernel(core_ref, back_ref, route0_ref, route1_ref, cot_ref, own_ref, other_ref, x_ref, m_ref, p_ref, o_ref, h_ref, b_ref, c_ref, y0_ref, c0_ref, out_ref, dx_ref, g_ref, buf_ref, dgv_ref, w_ref):
    unpack_weights(core_ref[0], own_ref, other_ref, w_ref)
    small, gain1, gain2 = unpack_small(own_ref)
    marks = routing(route1_ref)
    chance = c_ref[...]
    h = h_ref[...]
    z, y_both = combine(h, back_ref[:, :WIDTH], chance, marks)
    out_ref[...] = z.astype(BF)
    dz = cot_ref[...].astype(F32)
    dgv = gate_grads(dz, y_both, marks)
    dx = layer_backward(dz, back_ref[:, WIDTH:], marks, dgv, x_ref[...].astype(F32), h, b_ref[...], chance, small, gain1, gain2, w_ref, m_ref, p_ref, o_ref, g_ref)
    dx_ref[...] = dx
    dz = dx.astype(BF).astype(F32)
    marks = routing(route0_ref)
    buf_ref[...] = grad_rows(dz, c0_ref[...], marks)
    dgv_ref[...] = gate_grads(dz, y0_ref[...], marks)


def last_kernel(core_ref, back_ref, route_ref, dz_ref, dgv_ref, own_ref, other_ref, x_ref, m_ref, p_ref, o_ref, h_ref, b_ref, c_ref, dx_ref, g_ref, w_ref):
    unpack_weights(core_ref[0], own_ref, other_ref, w_ref)
    small, gain1, gain2 = unpack_small(own_ref)
    marks = routing(route_ref)
    dz = dz_ref[...].astype(BF).astype(F32)
    dx_ref[...] = layer_backward(dz, back_ref[...], marks, dgv_ref[...], x_ref[...].astype(F32), h_ref[...], b_ref[...], c_ref[...], small, gain1, gain2, w_ref, m_ref, p_ref, o_ref, g_ref)


def whole_call(kernel, name, outs, args):
    vmem = pl.BlockSpec(memory_space=pltpu.VMEM)
    return pl.pallas_call(
        kernel,
        name=name,
        out_shape=[jax.ShapeDtypeStruct(shape, dtype) for shape, dtype in outs],
        in_specs=[pl.BlockSpec(memory_space=pltpu.SMEM)] + [vmem] * (len(args) - 1),
        out_specs=[vmem] * len(outs),
        scratch_shapes=[pltpu.VMEM((ROWS, WIDTH, WIDTH), BF)],
        compiler_params=pltpu.CompilerParams(vmem_limit_bytes=VMEM),
    )(*args)


SAVED = [
    ((PAD, ROWS * 640), BF),
    ((ROWS * 3 * PAD, PAD), BF),
    ((PAD, ROWS * 256), BF),
    ((PAD, WIDTH), F32),
    ((PAD, WIDTH), BF),
    ((PAD, 128), F32),
]
GRADS = ((CHIPS, 6 * PART + 16, 128), BF)


def choose(core, section, own_first, other_first, own_second, other_second, first, second):
    @pl.when(core == section)
    def _():
        first[...] = own_first[...]
        second[...] = own_second[...]

    @pl.when(core != section)
    def _():
        first[...] = other_first[...]
        second[...] = other_second[...]


def expert_forward_kernel(section, core_ref, rows_ref, a_ref, b_ref, c_ref, d_ref, y_ref, q_ref, gp_ref, w1, w2, total):
    step = pl.program_id(0)
    choose(core_ref[0], section, a_ref, b_ref, c_ref, d_ref, w1, w2)
    q, gp = gelu_parts(dot(rows_ref[...], w1[...]))
    q = q.astype(BF)
    q_ref[...] = q
    gp_ref[...] = gp.astype(BF)
    part = dot(q, w2[...])

    @pl.when(step == 0)
    def _():
        total[...] = part

    @pl.when(step > 0)
    def _():
        total[...] += part

    @pl.when(step == pl.num_programs(0) - 1)
    def _():
        y_ref[...] = total[...].astype(BF)


def expert_both_kernel(section, core_ref, rows_ref, a_ref, b_ref, c_ref, d_ref, back_ref, g1_ref, g2_ref, w1, w2, total, total_back):
    step = pl.program_id(0)
    choose(core_ref[0], section, a_ref, b_ref, c_ref, d_ref, w1, w2)
    rows = rows_ref[:, :WIDTH]
    dy = rows_ref[:, WIDTH:]
    q, gp = gelu_parts(dot(rows, w1[...]))
    q = q.astype(BF)
    part = dot(q, w2[...])
    df = (dot_nt(dy, w2[...]) * gp).astype(BF)
    part_back = dot_nt(df, w1[...])
    g2_ref[...] = dot_tn(q, dy).astype(BF)
    g1_ref[...] = dot_tn(rows, df).astype(BF)

    @pl.when(step == 0)
    def _():
        total[...] = part
        total_back[...] = part_back

    @pl.when(step > 0)
    def _():
        total[...] += part
        total_back[...] += part_back

    @pl.when(step == pl.num_programs(0) - 1)
    def _():
        back_ref[:, :WIDTH] = total[...].astype(BF)
        back_ref[:, WIDTH:] = total_back[...].astype(BF)


def expert_backward_kernel(section, core_ref, rows_ref, dy_ref, q_ref, gp_ref, a_ref, b_ref, c_ref, d_ref, back_ref, g1_ref, g2_ref, w1, w2, total):
    step = pl.program_id(0)
    choose(core_ref[0], section, a_ref, b_ref, c_ref, d_ref, w1, w2)
    dy = dy_ref[...]
    df = (dot_nt(dy, w2[...]) * gp_ref[...].astype(F32)).astype(BF)
    part = dot_nt(df, w1[...])
    g2_ref[...] = dot_tn(q_ref[...], dy).astype(BF)
    g1_ref[...] = dot_tn(rows_ref[...], df).astype(BF)

    @pl.when(step == 0)
    def _():
        total[...] = part

    @pl.when(step > 0)
    def _():
        total[...] += part

    @pl.when(step == pl.num_programs(0) - 1)
    def _():
        back_ref[...] = total[...].astype(BF)


def expert_call(kernel, name, section, core, arrays, weights, outs, totals):
    def along(wanted, wide):
        def index(i, core_ref):
            here = (core_ref[0] == section) == wanted
            block = jnp.where(here, i, 0)
            return (0, block) if wide else (block, 0)

        return index

    def whole(shape):
        return pl.BlockSpec(shape, lambda i, core_ref: (0, 0))

    def wide(shape):
        return pl.BlockSpec((shape[0], STEP), lambda i, core_ref: (0, i))

    def tall(shape):
        return pl.BlockSpec((STEP, shape[1]), lambda i, core_ref: (i, 0))

    def spec(kind, shape):
        return {"whole": whole, "wide": wide, "tall": tall}[kind](shape)

    in_specs = [spec(kind, array.shape) for kind, array in arrays]
    in_specs += [
        pl.BlockSpec((WIDTH, STEP), along(True, True)),
        pl.BlockSpec((WIDTH, STEP), along(False, True)),
        pl.BlockSpec((STEP, WIDTH), along(True, False)),
        pl.BlockSpec((STEP, WIDTH), along(False, False)),
    ]
    return pl.pallas_call(
        functools.partial(kernel, section),
        name=name,
        out_shape=[jax.ShapeDtypeStruct(shape, BF) for _, shape in outs],
        grid_spec=pltpu.PrefetchScalarGridSpec(
            num_scalar_prefetch=1,
            grid=(HIDDEN // STEP,),
            in_specs=in_specs,
            out_specs=[spec(kind, shape) for kind, shape in outs],
            scratch_shapes=[pltpu.VMEM((WIDTH, STEP), BF), pltpu.VMEM((STEP, WIDTH), BF)]
            + [pltpu.VMEM((FILL, WIDTH), F32)] * totals,
        ),
        compiler_params=pltpu.CompilerParams(vmem_limit_bytes=VMEM),
    )(core, *[array for _, array in arrays], *weights)


def pair_sum_kernel(count, core_ref, *refs):
    for i in range(count):
        a, b, c, d = refs[4 * i : 4 * i + 4]
        out = refs[4 * count + i]

        @pl.when(core_ref[0] == 0)
        def _(a=a, b=b, out=out):
            out[...] = (a[...].astype(F32) + b[...].astype(F32)).astype(out.dtype)

        @pl.when(core_ref[0] == 1)
        def _(c=c, d=d, out=out):
            out[...] = (c[...].astype(F32) + d[...].astype(F32)).astype(out.dtype)


def pair_sum(name, core, groups, dtype, steps):
    def spec(shape, section):
        block = (shape[0] // steps,) + shape[1:]

        def index(i, core_ref):
            here = i if section is None else jnp.where(core_ref[0] == section, i, 0)
            return (here,) + (0,) * (len(shape) - 1)

        return pl.BlockSpec(block, index)

    return pl.pallas_call(
        functools.partial(pair_sum_kernel, len(groups)),
        name=name,
        out_shape=[jax.ShapeDtypeStruct(group[0].shape, dtype) for group in groups],
        grid_spec=pltpu.PrefetchScalarGridSpec(
            num_scalar_prefetch=1,
            grid=(steps,),
            in_specs=[spec(group[0].shape, section) for group in groups for section in (0, 0, 1, 1)],
            out_specs=[spec(group[0].shape, None) for group in groups],
        ),
        compiler_params=pltpu.CompilerParams(vmem_limit_bytes=VMEM),
    )(core, *[array for group in groups for array in group])


SWAP = [(0, 1), (1, 0)]
CHIP = ("row", "col")


def swap(values):
    return lax.ppermute(values, "section", SWAP)


def exchange(rows):
    wide = rows.shape[1]
    out = lax.all_to_all(
        rows.reshape(CHIPS, SLOTS, wide), CHIP, split_axis=0, concat_axis=0, tiled=True
    )
    return out.reshape(FILL, wide)


def gather_now(chunk):
    copies = jnp.broadcast_to(chunk[None], (CHIPS,) + chunk.shape)
    return lax.all_to_all(copies, CHIP, split_axis=0, concat_axis=0, tiled=True)


def gather_later(chunk):
    return lax.all_gather(chunk, CHIP, axis=0)


def reduce_all(partial):
    received = lax.all_to_all(partial, CHIP, split_axis=0, concat_axis=0, tiled=True)
    return jnp.sum(received.astype(F32), axis=0)


def pack(norm_gains, attn_qkv, attn_out, router):
    q, k, v = attn_qkv[0, :, 0], attn_qkv[0, :, 1], attn_qkv[0, :, 2]
    o = attn_out[0].T
    small = jnp.concatenate([router[0], norm_gains[0].T], axis=1)
    small = jnp.pad(small, ((0, 16 - SMALL), (0, 128 - EXPERTS - 2)))
    lo, hi = slice(0, 128), slice(128, 192)
    first = jnp.concatenate([q[:, lo], k[:, lo], v[:, lo], small], axis=0)
    mixed = jnp.concatenate([q[:, hi], k[:, hi]], axis=1)
    last = jnp.concatenate([v[:, hi], o[:, hi]], axis=1)
    second = jnp.concatenate([mixed, o[:, lo], last, small], axis=0)
    return first, second


def unpack(total):
    b = [total[i * PART : (i + 1) * PART] for i in range(6)]
    q = jnp.concatenate([b[0], b[3][:, :HEAD]], axis=1)
    k = jnp.concatenate([b[1], b[3][:, HEAD:]], axis=1)
    v = jnp.concatenate([b[2], b[5][:, :HEAD]], axis=1)
    o = jnp.concatenate([b[4], b[5][:, HEAD:]], axis=1).T
    small = total[6 * PART : 6 * PART + SMALL]
    gains = small[:, EXPERTS : EXPERTS + 2].T
    return gains[None], jnp.stack([q, k, v], axis=1)[None], o[None], small[None, :, :EXPERTS]


def body(images, cotangent, norm_gains, attn_qkv, attn_out, router, expert_in, expert_out, routes):
    section = lax.axis_index("section")
    core = section.astype(jnp.int32).reshape(1)
    on_first = section == 0

    first, second = pack(norm_gains, attn_qkv, attn_out, router)
    mine = jnp.where(on_first, first, second)
    theirs = swap(jnp.where(on_first, second, first))
    own0 = gather_now(jnp.where(on_first, mine, theirs))
    other0 = swap(own0)
    own1 = gather_later(jnp.where(on_first, theirs, mine))
    other1 = swap(own1)

    w1, w2 = expert_in[0], expert_out[0]
    w1_other, w2_other = swap(w1), swap(w2)
    weights = (w1, w1_other, w2, w2_other)

    def tokens(values):
        mine = lax.dynamic_index_in_dim(values, section, 0, keepdims=False)
        return jnp.pad(mine.reshape(TOKENS, WIDTH), ((0, PAD - TOKENS), (0, 0)))

    x0 = tokens(images)
    cot = tokens(cotangent)
    chosen = routes[0].reshape(2, TOKENS, 2)
    chosen = jnp.pad(chosen, ((0, 0), (0, PAD - TOKENS), (0, 126)), constant_values=-1)
    kept = jnp.where(on_first, chosen[0], chosen[1])
    got = swap(jnp.where(on_first, chosen[1], chosen[0]))
    route0 = jnp.where(on_first, kept, got)
    route1 = jnp.where(on_first, got, kept)

    buf_shape = ((FILL, WIDTH), BF)
    wide_shape = ((FILL, 2 * WIDTH), BF)
    tok_b = ((PAD, WIDTH), BF)
    tok_f = ((PAD, WIDTH), F32)

    buf, *saved0 = whole_call(
        first_kernel, "first", [buf_shape] + SAVED, (core, x0, route0, own0, other0)
    )
    rows0 = exchange(buf)
    y, q0, gp0 = expert_call(
        expert_forward_kernel, "expert_forward", 0, core, [("whole", rows0)], weights,
        [("whole", (FILL, WIDTH)), ("wide", (FILL, HIDDEN)), ("wide", (FILL, HIDDEN))], 1,
    )
    back = exchange(y)
    h0, c0 = saved0[3], saved0[5]
    x1, y_both, buf, *saved1 = whole_call(
        middle_kernel, "middle", [tok_b, ((PAD, 2 * WIDTH), BF), wide_shape] + SAVED,
        (core, back, h0, c0, route0, route1, cot, own1, other1),
    )
    rows1 = exchange(buf)
    back, g1_1, g2_1 = expert_call(
        expert_both_kernel, "expert_both", 1, core, [("whole", rows1)], weights,
        [("whole", (FILL, 2 * WIDTH)), ("wide", (WIDTH, HIDDEN)), ("tall", (HIDDEN, WIDTH))], 2,
    )
    back = exchange(back)
    to_second, to_first = [(0, 1)], [(1, 0)]
    r1_1 = lax.ppermute(g1_1, "section", to_second)
    r2_1 = lax.ppermute(g2_1, "section", to_second)
    out1, dx1, ga1, buf, dgv = whole_call(
        turn_kernel, "turn", [tok_b, tok_f, GRADS, buf_shape, ((PAD, 128), F32)],
        (core, back, route0, route1, cot, own1, other1, x1, *saved1, y_both, c0),
    )
    dy0 = exchange(buf)
    ra1 = lax.ppermute(ga1, "section", to_second)
    back, g1_0, g2_0 = expert_call(
        expert_backward_kernel, "expert_backward", 0, core,
        [("whole", rows0), ("whole", dy0), ("wide", q0), ("wide", gp0)], weights,
        [("whole", (FILL, WIDTH)), ("wide", (WIDTH, HIDDEN)), ("tall", (HIDDEN, WIDTH))], 1,
    )
    back = exchange(back)
    r1_0 = lax.ppermute(g1_0, "section", to_first)
    r2_0 = lax.ppermute(g2_0, "section", to_first)
    dx0, ga0 = whole_call(
        last_kernel, "last", [tok_f, GRADS],
        (core, back, route0, dx1, dgv, own0, other0, x0, *saved0),
    )
    ra0 = lax.ppermute(ga0, "section", to_first)
    (partial,) = pair_sum("sum_small", core, [(ga0, ra0, ga1, ra1)], BF, 4)
    total = reduce_all(partial)
    grad_first, grad_second = pair_sum(
        "sum_experts", core, [(g1_0, r1_0, g1_1, r1_1), (g2_0, r2_0, g2_1, r2_1)], F32, 6
    )

    def place(value0, value1):
        kept = jnp.where(on_first, value0, value1)
        got = swap(jnp.where(on_first, value1, value0))
        both = jnp.stack([jnp.where(on_first, kept, got), jnp.where(on_first, got, kept)])
        return both[:, :TOKENS].reshape(1, 2, 2, SEQ, WIDTH)

    section_out = place(x1, out1)
    input_grads = place(dx0, dx1)
    gains, qkv, out, rout = unpack(total)
    return (section_out, input_grads, gains, qkv, out, rout, grad_first[None], grad_second[None])


def solution(mesh):
    in_specs = (
        P(None, ("row", "col"), None, None),
        P(None, ("row", "col"), None, None),
        P("section", None, ("row", "col")),
        P("section", "col", None, "row"),
        P("section", "row", "col"),
        P("section", ("row", "col"), None),
        P("section", None, ("row", "col")),
        P("section", ("row", "col"), None),
        P("section", None, ("row", "col"), None, None),
    )
    out_specs = (
        P("section", None, ("row", "col"), None, None),
        P("section", None, ("row", "col"), None, None),
        P("section", None, ("row", "col")),
        P("section", "col", None, "row"),
        P("section", "row", "col"),
        P("section", ("row", "col"), None),
        P("section", None, ("row", "col")),
        P("section", ("row", "col"), None),
    )
    return jax.shard_map(body, mesh=mesh, in_specs=in_specs, out_specs=out_specs, check_vma=False)
```

```python
import functools

import jax
import jax.numpy as jnp
from jax import lax
from jax.experimental import pallas as pl
from jax.experimental.pallas import tpu as pltpu
from jax.sharding import PartitionSpec as P

HEAD = 64
WIDTH = 768
SEQ = 50
SPAN = 56
PAD = 2 * SPAN
EXPERTS = 32
SLOTS = 8
ROWS = 4
COLS = 16
CHIPS = ROWS * COLS
PART = WIDTH // COLS
SMALL = WIDTH // CHIPS
FILL = CHIPS * SLOTS
HIDDEN = 1536
STEP = 512
EPSILON = 1e-06
SCALE = float(HEAD) ** (-0.5)
VMEM = 58 * 1024 * 1024
BF = jnp.bfloat16
F32 = jnp.float32


def dot(left, right):
    return jnp.dot(left, right, preferred_element_type=F32)


def dot_tn(left, right):
    return lax.dot_general(left, right, (((0,), (0,)), ((), ())), preferred_element_type=F32)


def dot_nt(left, right):
    return lax.dot_general(left, right, (((1,), (1,)), ((), ())), preferred_element_type=F32)


def iota(shape, axis):
    return lax.broadcasted_iota(jnp.int32, shape, axis)


def hot(flag):
    return jnp.where(flag, 1.0, 0.0)


def normalise(values):
    centred = values - jnp.mean(values, axis=-1, keepdims=True)
    spread = jnp.mean(centred * centred, axis=-1, keepdims=True)
    inverse = lax.rsqrt(spread + EPSILON)
    return centred * inverse, inverse


def normalise_back(grad, unit, inverse):
    return inverse * (
        grad
        - jnp.mean(grad, axis=-1, keepdims=True)
        - unit * jnp.mean(grad * unit, axis=-1, keepdims=True)
    )


def gelu_parts(values):
    bell = jnp.exp(-0.5 * values * values)
    t = 1.0 / (1.0 + (0.3275911 * 0.7071067811865476) * jnp.abs(values))
    poly = 1.061405429 * t - 1.453152027
    poly = poly * t + 1.421413741
    poly = poly * t - 0.284496736
    poly = poly * t + 0.254829592
    tail = (0.5 * t) * poly * bell
    below = jnp.where(values < 0, tail, 1.0 - tail)
    return values * below, below + values * (0.3989422804014327 * bell)


def half_turn(values):
    return pltpu.roll(values, HEAD, 1)


def lane_low(rows):
    return iota((rows, 2 * HEAD), 1) < HEAD


def weight_reader(core, own_ref, other_ref, w_ref, small_ref, sems):
    small_copy = pltpu.make_async_copy(own_ref.at[:, 3 * PART : 3 * PART + 16, :], small_ref, sems.at[6, 0])
    small_copy.start()

    def copy(ref, half, r, b):
        at = (3 * half + b) * 128
        return pltpu.make_async_copy(
            ref.at[r * COLS : (r + 1) * COLS, b * PART : (b + 1) * PART, :],
            w_ref.at[r, :, :, at : at + 128],
            sems.at[3 * half + b, r],
        )

    def start(refs):
        for r in range(ROWS):
            for half in range(2):
                for b in range(3):
                    copy(refs[half], half, r, b).start()

    @pl.when(core == 0)
    def _():
        start((own_ref, other_ref))

    @pl.when(core == 1)
    def _():
        start((other_ref, own_ref))

    def wait():
        for r in range(ROWS):
            for half in range(2):
                for b in range(3):
                    copy(own_ref, half, r, b).wait()

    def read(r, first, last):
        return w_ref[r, :, :, first:last].reshape(WIDTH, last - first)

    return small_copy.wait, wait, read


def small_places():
    inside = iota((WIDTH, CHIPS * 16), 1)
    group = lax.shift_right_logical(inside, 4)
    place = jnp.bitwise_and(inside, 15)
    wanted = group * SMALL + place
    return hot((iota((WIDTH, CHIPS * 16), 0) == wanted) & (place < SMALL)).astype(BF)


def unpack_small(small_ref):
    packed = small_ref[...].reshape(CHIPS * 16, 128)
    small = dot(small_places(), packed).astype(BF)
    pick = hot(iota((8, 128), 1) == iota((8, 128), 0) + EXPERTS).astype(BF)
    gains = dot_nt(pick, small)
    return small, gains[0:1], gains[1:2]


def routing(core, section, own_ref, other_ref):
    chosen = jnp.where(core == section, own_ref[core], other_ref[core])
    first = chosen[:, 0:1]
    second = chosen[:, 1:2]
    lane = iota((PAD, 128), 1)
    hot0 = hot(lane == first)
    hot1 = hot(lane == second)
    before = hot(iota((PAD, PAD), 0) > iota((PAD, PAD), 1)).astype(BF)
    earlier = dot(before, (hot0 + hot1).astype(BF))
    place = iota((PAD, FILL), 1)

    def spread(expert, marks):
        slot = jnp.sum(earlier * marks, axis=1, keepdims=True).astype(jnp.int32)
        base = expert * (2 * SLOTS) + slot
        return hot((place == base) | (place == base + SLOTS)).astype(BF)

    return hot0, hot1, spread(first, hot0), spread(second, hot1)


def gates(chance, marks):
    return jnp.sum(chance * marks, axis=1, keepdims=True)


def image_bias():
    query = iota((PAD, PAD), 0)
    key = iota((PAD, PAD), 1)
    first = (query < SPAN) & (key < SEQ)
    second = (query >= SPAN) & (key >= SPAN) & (key < SPAN + SEQ)
    bias = jnp.where(first | second, 0.0, -1e30)
    return jnp.concatenate([bias] * 3, axis=0)


def read_tokens(ref):
    blank = jnp.zeros((SPAN - SEQ, WIDTH), F32)
    return jnp.concatenate([ref[0].astype(F32), blank, ref[1].astype(F32), blank], axis=0)


def write_tokens(ref, values):
    ref[0] = values[:SEQ].astype(ref.dtype)
    ref[1] = values[SPAN : SPAN + SEQ].astype(ref.dtype)


def attention_forward(x, wait, read, gain, m_ref, p_ref, o_ref):
    unit, _ = normalise(x)
    a = (unit * gain).astype(BF)
    low = lane_low(PAD)
    low_b = hot(low).astype(BF)
    high_b = (1.0 - hot(low)).astype(BF)
    bias = image_bias()
    branch = jnp.zeros((PAD, WIDTH), F32)
    wait()
    for r in range(ROWS):
        wide = dot(a, read(r, 0, 512))
        m5 = dot(a, read(r, 640, 768)).astype(BF)
        m = wide.astype(BF)
        m_ref[:, r * 640 : r * 640 + 512] = m
        m_ref[:, r * 640 + 512 : r * 640 + 640] = m5
        q, k, v, qk = m[:, 0:128], m[:, 128:256], m[:, 256:384], m[:, 384:512]
        k2 = half_turn(wide[:, 384:512]).astype(BF)
        qs = jnp.concatenate([q * low_b, q * high_b], axis=0)
        s = jnp.concatenate([dot_nt(qs, k), dot_nt(qk * low_b, k2)], axis=0)
        s = s * SCALE + bias
        e = jnp.exp(s - jnp.max(s, axis=-1, keepdims=True))
        p = (e / jnp.sum(e, axis=-1, keepdims=True)).astype(BF)
        p_ref[r * 3 * PAD : (r + 1) * 3 * PAD, :] = p
        os = dot(p[: 2 * PAD], v)
        o2 = dot(p[2 * PAD :], m5)
        o01 = jnp.where(low, os[:PAD], os[PAD:])
        o2 = jnp.where(low, 0.0, half_turn(o2))
        o = jnp.concatenate([o01, o2], axis=1).astype(BF)
        o_ref[:, r * 256 : (r + 1) * 256] = o
        branch = branch + dot_nt(o, read(r, 512, 768))
    return x + branch


def route_forward(h, small, gain):
    unit, _ = normalise(h)
    b = (unit * gain).astype(BF)
    logits = dot(b, small)
    inside = iota((PAD, 128), 1) < EXPERTS
    logits = jnp.where(inside, logits, -1e30)
    e = jnp.exp(logits - jnp.max(logits, axis=-1, keepdims=True))
    e = jnp.where(inside, e, 0.0)
    return b, e / jnp.sum(e, axis=-1, keepdims=True)


def attention_backward(dh, x, gain, wait, read, m_ref, p_ref, o_ref, g_ref, ship):
    db = dh.astype(BF)
    unit, inverse = normalise(x)
    a = (unit * gain).astype(BF)
    low = lane_low(PAD)
    low_b = hot(low).astype(BF)
    high_b = (1.0 - hot(low)).astype(BF)
    da = jnp.zeros((PAD, WIDTH), F32)
    wait()
    for r in range(ROWS):
        o = o_ref[:, r * 256 : (r + 1) * 256]
        q = m_ref[:, r * 640 : r * 640 + 128]
        k = m_ref[:, r * 640 + 128 : r * 640 + 256]
        v = m_ref[:, r * 640 + 256 : r * 640 + 384]
        qk = m_ref[:, r * 640 + 384 : r * 640 + 512]
        m5 = m_ref[:, r * 640 + 512 : r * 640 + 640]
        k2 = half_turn(qk.astype(F32)).astype(BF)
        q2 = qk * low_b
        qs = jnp.concatenate([q * low_b, q * high_b], axis=0)
        pb = p_ref[r * 3 * PAD : (r + 1) * 3 * PAD, :]
        p = pb.astype(F32)
        do = dot(db, read(r, 512, 768))
        do01 = do[:, 0:128].astype(BF)
        do2 = half_turn(do[:, 128:256]).astype(BF) * low_b
        dos = jnp.concatenate([do01 * low_b, do01 * high_b], axis=0)
        dp = jnp.concatenate([dot_nt(dos, v), dot_nt(do2, m5)], axis=0)
        ds = (p * (dp - jnp.sum(dp * p, axis=-1, keepdims=True))).astype(BF)
        dv = dot_tn(pb[: 2 * PAD], dos)
        dv2 = dot_tn(pb[2 * PAD :], do2)
        dqs = dot(ds[: 2 * PAD], k)
        dq = jnp.where(low, dqs[:PAD], dqs[PAD:]) * SCALE
        dk = dot_tn(ds[: 2 * PAD], qs) * SCALE
        dq2 = dot(ds[2 * PAD :], k2) * SCALE
        dk2 = dot_tn(ds[2 * PAD :], q2) * SCALE
        dqk = jnp.where(low, dq2, half_turn(dk2))
        dm = jnp.concatenate([dq, dk, dv, dqk, dv2], axis=1).astype(BF)
        da = da + dot_nt(dm[:, :512], read(r, 0, 512)) + dot_nt(dm[:, 512:], read(r, 640, 768))
        gm = dot_tn(a, dm)
        go = dot_tn(db, o)
        blocks = [gm[:, i * 128 : (i + 1) * 128] for i in range(4)]
        blocks += [go[:, :128], gm[:, 512:640] + go[:, 128:256]]
        for i, block in enumerate(blocks):
            at = i % 3 * PART
            g_ref[i // 3, r * COLS : (r + 1) * COLS, at : at + PART, :] = block.astype(BF).reshape(
                COLS, PART, 128
            )
    for r in range(ROWS):
        ship(r)
    dx = dh + normalise_back(da * gain, unit, inverse)
    return dx, (da * unit).astype(BF)


def layer_backward(dz, dr, marks, dgv, x, h, b, chance, small, gain1, gain2, wait, read, m_ref, p_ref, o_ref, g_ref, ship):
    _, _, d0, d1 = marks
    dn = dot(d0, dr).astype(BF).astype(F32) + dot(d1, dr).astype(BF).astype(F32)
    dl = (chance * (dgv - jnp.sum(dgv * chance, axis=1, keepdims=True))).astype(BF)
    dn = dn + dot_nt(dl, small)
    unit, inverse = normalise(h)
    dh = dz + normalise_back(dn * gain2, unit, inverse)
    dx, terms = attention_backward(dh, x, gain1, wait, read, m_ref, p_ref, o_ref, g_ref, ship)
    lane = iota((PAD, 128), 1)
    gs = dot_tn(b, dl)
    gs = gs + dot_tn(terms, hot(lane == EXPERTS).astype(BF))
    gs = gs + dot_tn((dn * unit).astype(BF), hot(lane == EXPERTS + 1).astype(BF))
    spread = dot_tn(small_places(), gs.astype(BF)).astype(BF)
    spread = spread.reshape(CHIPS, 16, 128)
    g_ref[0, :, 3 * PART :, :] = spread
    g_ref[1, :, 3 * PART :, :] = spread
    ship(ROWS)
    return dx


def shipping(core, g_ref, keep_ref, send_ref, sems):
    copies = []

    def ship(r):
        if r < ROWS:
            here = (slice(r * COLS, (r + 1) * COLS), slice(0, 3 * PART))
        else:
            here = (slice(0, CHIPS), slice(3 * PART, 3 * PART + 16))
        for i, (half, ref) in enumerate(((core, keep_ref), (1 - core, send_ref))):
            copies.append(pltpu.make_async_copy(g_ref.at[(half,) + here], ref.at[here], sems.at[i, r]))
            copies[-1].start()

    def finish():
        for copy in copies:
            copy.wait()

    return ship, finish


def gate_grads(dz, y_both, marks):
    hot0, hot1 = marks[0], marks[1]
    dg0 = jnp.sum(dz * y_both[:, :WIDTH].astype(F32), axis=1, keepdims=True)
    dg1 = jnp.sum(dz * y_both[:, WIDTH:].astype(F32), axis=1, keepdims=True)
    return dg0 * hot0 + dg1 * hot1


def grad_rows(dz, chance, marks):
    hot0, hot1, d0, d1 = marks
    dy0 = (gates(chance, hot0) * dz).astype(BF)
    dy1 = (gates(chance, hot1) * dz).astype(BF)
    return (dot_tn(d0, dy0) + dot_tn(d1, dy1)).astype(BF)


def combine(h, returned, chance, marks):
    hot0, hot1, d0, d1 = marks
    y0 = dot(d0, returned).astype(BF)
    y1 = dot(d1, returned).astype(BF)
    z = h + gates(chance, hot0) * y0.astype(F32) + gates(chance, hot1) * y1.astype(F32)
    return z, jnp.concatenate([y0, y1], axis=1)


def first_kernel(core_ref, x_ref, routes_ref, routes_other_ref, own_ref, other_ref, buf_ref, m_ref, p_ref, o_ref, h_ref, b_ref, c_ref, w_ref, small_ref, w_sems):
    core = core_ref[0]
    ready, wait, read = weight_reader(core, own_ref, other_ref, w_ref, small_ref, w_sems)
    ready()
    small, gain1, gain2 = unpack_small(small_ref)
    marks = routing(core, 0, routes_ref, routes_other_ref)
    h = attention_forward(read_tokens(x_ref.at[core]), wait, read, gain1, m_ref, p_ref, o_ref)
    b, chance = route_forward(h, small, gain2)
    h_ref[...] = h
    b_ref[...] = b
    c_ref[...] = chance
    buf_ref[...] = dot_tn(marks[2] + marks[3], b).astype(BF)


def middle_kernel(core_ref, back_ref, h0_ref, c0_ref, routes_ref, routes_other_ref, cot_ref, own_ref, other_ref, x_ref, y_ref, buf_ref, m_ref, p_ref, o_ref, h_ref, b_ref, c_ref, w_ref, small_ref, w_sems):
    core = core_ref[0]
    ready, wait, read = weight_reader(core, own_ref, other_ref, w_ref, small_ref, w_sems)
    marks = routing(core, 0, routes_ref, routes_other_ref)
    z, y_both = combine(h0_ref[...], back_ref[...], c0_ref[...], marks)
    write_tokens(x_ref, z)
    y_ref[...] = y_both
    ready()
    small, gain1, gain2 = unpack_small(small_ref)
    marks = routing(core, 1, routes_ref, routes_other_ref)
    x = read_tokens(x_ref)
    h = attention_forward(x, wait, read, gain1, m_ref, p_ref, o_ref)
    b, chance = route_forward(h, small, gain2)
    h_ref[...] = h
    b_ref[...] = b
    c_ref[...] = chance
    buf_ref[:, :WIDTH] = dot_tn(marks[2] + marks[3], b).astype(BF)
    buf_ref[:, WIDTH:] = grad_rows(read_tokens(cot_ref.at[core]), chance, marks)


def turn_kernel(core_ref, back_ref, routes_ref, routes_other_ref, cot_ref, x_ref, m_ref, p_ref, o_ref, h_ref, b_ref, c_ref, y0_ref, c0_ref, own_ref, other_ref, keep_ref, send_ref, dx_ref, gk_ref, gs_ref, buf_ref, dgv_ref, w_ref, small_ref, w_sems, g_ref, sems):
    core = core_ref[0]
    ready, wait, read = weight_reader(core, own_ref, other_ref, w_ref, small_ref, w_sems)
    ship, finish = shipping(core, g_ref, gk_ref, gs_ref, sems)
    ready()
    small, gain1, gain2 = unpack_small(small_ref)
    marks = routing(core, 1, routes_ref, routes_other_ref)
    chance = c_ref[...]
    h = h_ref[...]
    z, y_both = combine(h, back_ref[:, :WIDTH], chance, marks)
    x = read_tokens(x_ref)
    on_first = core == 0
    write_tokens(keep_ref, jnp.where(on_first, x, z))
    write_tokens(send_ref, jnp.where(on_first, z, x))
    dz = read_tokens(cot_ref.at[core])
    dgv = gate_grads(dz, y_both, marks)
    dx = layer_backward(dz, back_ref[:, WIDTH:], marks, dgv, x, h, b_ref[...], chance, small, gain1, gain2, wait, read, m_ref, p_ref, o_ref, g_ref, ship)
    dx_ref[...] = dx
    dz = dx.astype(BF).astype(F32)
    marks = routing(core, 0, routes_ref, routes_other_ref)
    buf_ref[...] = grad_rows(dz, c0_ref[...], marks)
    dgv_ref[...] = gate_grads(dz, y0_ref[...], marks)
    finish()


def last_kernel(core_ref, back_ref, routes_ref, routes_other_ref, dz_ref, dgv_ref, x_ref, m_ref, p_ref, o_ref, h_ref, b_ref, c_ref, own_ref, other_ref, keep_ref, send_ref, gk_ref, gs_ref, w_ref, small_ref, w_sems, g_ref, sems):
    core = core_ref[0]
    ready, wait, read = weight_reader(core, own_ref, other_ref, w_ref, small_ref, w_sems)
    ship, finish = shipping(core, g_ref, gk_ref, gs_ref, sems)
    ready()
    small, gain1, gain2 = unpack_small(small_ref)
    marks = routing(core, 0, routes_ref, routes_other_ref)
    dx1 = dz_ref[...]
    dz = dx1.astype(BF).astype(F32)
    dx = layer_backward(dz, back_ref[...], marks, dgv_ref[...], read_tokens(x_ref.at[core]), h_ref[...], b_ref[...], c_ref[...], small, gain1, gain2, wait, read, m_ref, p_ref, o_ref, g_ref, ship)
    on_first = core == 0
    write_tokens(keep_ref, jnp.where(on_first, dx, dx1))
    write_tokens(send_ref, jnp.where(on_first, dx1, dx))
    finish()


def whole_call(kernel, name, outs, args, weights):
    vmem = pl.BlockSpec(memory_space=pltpu.VMEM)
    far = pl.BlockSpec(memory_space=pl.ANY)
    scratch = [
        pltpu.VMEM((ROWS, COLS, PART, WIDTH), BF),
        pltpu.VMEM((CHIPS, 16, 128), BF),
        pltpu.SemaphoreType.DMA((7, ROWS)),
    ]
    if GRADS in outs:
        scratch += [pltpu.VMEM((2,) + GRADS[0], BF), pltpu.SemaphoreType.DMA((2, ROWS + 1))]
    return pl.pallas_call(
        kernel,
        name=name,
        out_shape=[jax.ShapeDtypeStruct(shape, dtype) for shape, dtype in outs],
        in_specs=[pl.BlockSpec(memory_space=pltpu.SMEM)] + [vmem] * (len(args) - 1) + [far] * 2,
        out_specs=[far if out == GRADS else vmem for out in outs],
        scratch_shapes=scratch,
        compiler_params=pltpu.CompilerParams(vmem_limit_bytes=VMEM),
    )(*args, *weights)


SAVED = [
    ((PAD, ROWS * 640), BF),
    ((ROWS * 3 * PAD, PAD), BF),
    ((PAD, ROWS * 256), BF),
    ((PAD, WIDTH), F32),
    ((PAD, WIDTH), BF),
    ((PAD, 128), F32),
]
GRADS = ((CHIPS, 3 * PART + 16, 128), BF)


def fetch(core, section, own_refs, other_refs, places, sems):
    def start(refs):
        for j in range(HIDDEN // STEP):
            here = slice(j * STEP, (j + 1) * STEP)
            pltpu.make_async_copy(refs[0].at[:, here], places[0].at[:, here], sems.at[0, j]).start()
            pltpu.make_async_copy(refs[1].at[here, :], places[1].at[here, :], sems.at[1, j]).start()

    @pl.when(core == section)
    def _():
        start(own_refs)

    @pl.when(core != section)
    def _():
        start(other_refs)


def fetched(own_refs, places, sems, j):
    here = slice(j * STEP, (j + 1) * STEP)
    pltpu.make_async_copy(own_refs[0].at[:, here], places[0].at[:, here], sems.at[0, j]).wait()
    pltpu.make_async_copy(own_refs[1].at[here, :], places[1].at[here, :], sems.at[1, j]).wait()


def add_to(total, j, value):
    total[...] = value if j == 0 else total[...] + value


def send(pairs):
    copies = [pltpu.make_async_copy(*pair) for pair in pairs]
    for copy in copies:
        copy.start()
    return copies


def expert_forward_kernel(section, core_ref, rows_ref, a_ref, b_ref, c_ref, d_ref, y_ref, q_ref, gp_ref, w1, w2, sems, total, q_s, gp_s, out_sems):
    fetch(core_ref[0], section, (a_ref, c_ref), (b_ref, d_ref), (w1, w2), sems)
    copies = []
    for j in range(HIDDEN // STEP):
        fetched((a_ref, c_ref), (w1, w2), sems, j)
        here = slice(j * STEP, (j + 1) * STEP)
        q, gp = gelu_parts(dot(rows_ref[...], w1[:, here]))
        q = q.astype(BF)
        q_s[:, here] = q
        gp_s[:, here] = gp.astype(BF)
        add_to(total, j, dot(q, w2[here, :]))
        copies += send([
            (q_s.at[:, here], q_ref.at[:, here], out_sems.at[0, j]),
            (gp_s.at[:, here], gp_ref.at[:, here], out_sems.at[1, j]),
        ])
    y_ref[...] = total[...].astype(BF)
    for copy in copies:
        copy.wait()


def expert_both_kernel(section, core_ref, rows_ref, a_ref, b_ref, c_ref, d_ref, back_ref, g1_ref, g2_ref, w1, w2, sems, total, total_back, turned, g1_s, g2_s, out_sems):
    fetch(core_ref[0], section, (a_ref, c_ref), (b_ref, d_ref), (w1, w2), sems)
    turned[...] = rows_ref[:, :WIDTH].T
    copies = []
    for j in range(HIDDEN // STEP):
        fetched((a_ref, c_ref), (w1, w2), sems, j)
        here = slice(j * STEP, (j + 1) * STEP)
        q, gp = gelu_parts(dot(rows_ref[:, :WIDTH], w1[:, here]))
        q = q.astype(BF)
        df = (dot_nt(rows_ref[:, WIDTH:], w2[here, :]) * gp).astype(BF)
        add_to(total, j, dot(q, w2[here, :]))
        add_to(total_back, j, dot_nt(df, w1[:, here]))
        g2_s[here, :] = dot_tn(q, rows_ref[:, WIDTH:]).astype(BF)
        g1_s[:, here] = dot(turned[...], df).astype(BF)
        copies += send([
            (g1_s.at[:, here], g1_ref.at[:, here], out_sems.at[0, j]),
            (g2_s.at[here, :], g2_ref.at[here, :], out_sems.at[1, j]),
        ])
    back_ref[:, :WIDTH] = total[...].astype(BF)
    back_ref[:, WIDTH:] = total_back[...].astype(BF)
    for copy in copies:
        copy.wait()


def expert_backward_kernel(section, core_ref, rows_ref, dy_ref, a_ref, b_ref, c_ref, d_ref, q_far, gp_far, back_ref, g1_ref, g2_ref, w1, w2, sems, total, turned, g1_s, g2_s, out_sems, q_ref, gp_ref, in_sems):
    fetch(core_ref[0], section, (a_ref, c_ref), (b_ref, d_ref), (w1, w2), sems)
    kept = []
    for j in range(HIDDEN // STEP):
        here = slice(j * STEP, (j + 1) * STEP)
        kept.append(send([
            (gp_far.at[:, here], gp_ref.at[:, here], in_sems.at[0, j]),
            (q_far.at[:, here], q_ref.at[:, here], in_sems.at[1, j]),
        ]))
    turned[...] = rows_ref[...].T
    copies = []
    for j in range(HIDDEN // STEP):
        here = slice(j * STEP, (j + 1) * STEP)
        fetched((a_ref, c_ref), (w1, w2), sems, j)
        for copy in kept[j]:
            copy.wait()
        df = (dot_nt(dy_ref[...], w2[here, :]) * gp_ref[:, here].astype(F32)).astype(BF)
        add_to(total, j, dot_nt(df, w1[:, here]))
        g2_s[here, :] = dot_tn(q_ref[:, here], dy_ref[...]).astype(BF)
        g1_s[:, here] = dot(turned[...], df).astype(BF)
        copies += send([
            (g1_s.at[:, here], g1_ref.at[:, here], out_sems.at[0, j]),
            (g2_s.at[here, :], g2_ref.at[here, :], out_sems.at[1, j]),
        ])
    back_ref[...] = total[...].astype(BF)
    for copy in copies:
        copy.wait()


def expert_call(kernel, name, section, core, arrays, weights, outs, kept=()):
    vmem = pl.BlockSpec(memory_space=pltpu.VMEM)
    far = pl.BlockSpec(memory_space=pl.ANY)
    rows_f = pltpu.VMEM((FILL, WIDTH), F32)
    hid = pltpu.VMEM((FILL, HIDDEN), BF)
    first, second = pltpu.VMEM((WIDTH, HIDDEN), BF), pltpu.VMEM((HIDDEN, WIDTH), BF)
    sems = pltpu.SemaphoreType.DMA((2, HIDDEN // STEP))
    turned = pltpu.VMEM((WIDTH, FILL), BF)
    scratch = {
        "expert_forward": [first, second, sems, rows_f, hid, hid, sems],
        "expert_both": [first, second, sems, rows_f, rows_f, turned, first, second, sems],
        "expert_backward": [first, second, sems, rows_f, turned, first, second, sems, hid, hid, sems],
    }[name]
    return pl.pallas_call(
        functools.partial(kernel, section),
        name=name,
        out_shape=[jax.ShapeDtypeStruct(shape, BF) for shape in outs],
        in_specs=[pl.BlockSpec(memory_space=pltpu.SMEM)] + [vmem] * len(arrays) + [far] * (4 + len(kept)),
        out_specs=[vmem] + [far] * (len(outs) - 1),
        scratch_shapes=scratch,
        compiler_params=pltpu.CompilerParams(vmem_limit_bytes=VMEM),
    )(core, *arrays, *weights, *kept)


def pair_sum_kernel(count, core_ref, *refs):
    for i in range(count):
        a, b, c, d = refs[4 * i : 4 * i + 4]
        out = refs[4 * count + i]

        @pl.when(core_ref[0] == 0)
        def _(a=a, b=b, out=out):
            out[...] = (a[...].astype(F32) + b[...].astype(F32)).astype(out.dtype)

        @pl.when(core_ref[0] == 1)
        def _(c=c, d=d, out=out):
            out[...] = (c[...].astype(F32) + d[...].astype(F32)).astype(out.dtype)


def pair_sum(name, core, groups, dtype, steps):
    def spec(shape, section):
        block = (shape[0] // steps,) + shape[1:]

        def index(i, core_ref):
            here = i if section is None else jnp.where(core_ref[0] == section, i, 0)
            return (here,) + (0,) * (len(shape) - 1)

        return pl.BlockSpec(block, index)

    return pl.pallas_call(
        functools.partial(pair_sum_kernel, len(groups)),
        name=name,
        out_shape=[jax.ShapeDtypeStruct(group[0].shape, dtype) for group in groups],
        grid_spec=pltpu.PrefetchScalarGridSpec(
            num_scalar_prefetch=1,
            grid=(steps,),
            in_specs=[spec(group[0].shape, section) for group in groups for section in (0, 0, 1, 1)],
            out_specs=[spec(group[0].shape, None) for group in groups],
        ),
        compiler_params=pltpu.CompilerParams(vmem_limit_bytes=VMEM),
    )(core, *[array for group in groups for array in group])


SWAP = [(0, 1), (1, 0)]
CHIP = ("row", "col")


def swap(values):
    return lax.ppermute(values, "section", SWAP)


def exchange(rows):
    wide = rows.shape[1]
    out = lax.all_to_all(
        rows.reshape(CHIPS, SLOTS, wide), CHIP, split_axis=0, concat_axis=0, tiled=True
    )
    return out.reshape(FILL, wide)


def gather_now(chunk):
    copies = jnp.broadcast_to(chunk[None], (CHIPS,) + chunk.shape)
    return lax.all_to_all(copies, CHIP, split_axis=0, concat_axis=0, tiled=True)


def gather_later(chunk):
    return lax.all_gather(chunk, CHIP, axis=0)


def spread_out(partial):
    return lax.all_to_all(partial, CHIP, split_axis=0, concat_axis=0, tiled=True)


def reduce_step(chunks, mine, stride):
    side = 4
    total = lax.dynamic_index_in_dim(chunks, mine, 0, keepdims=False).astype(F32)
    for turn in range(1, side):
        pairs = []
        for at in range(COLS):
            own = at // stride % side
            pairs.append((at, at + ((own + turn) % side - own) * stride))
        chunk = lax.dynamic_index_in_dim(chunks, (mine + turn) % side, 0, keepdims=False)
        total = total + lax.ppermute(chunk, "col", pairs).astype(F32)
    return total


def reduce_x(values):
    place = lax.axis_index("col")
    chunks = values.reshape((4, 4) + values.shape[1:])
    return reduce_step(chunks, place // 4, 4).astype(BF), place % 4


def add_up(received):
    return jnp.sum(received.astype(F32), axis=0)


def pack(norm_gains, attn_qkv, attn_out, router):
    q, k, v = attn_qkv[0, :, 0], attn_qkv[0, :, 1], attn_qkv[0, :, 2]
    o = attn_out[0].T
    small = jnp.concatenate([router[0], norm_gains[0].T], axis=1)
    small = jnp.pad(small, ((0, 16 - SMALL), (0, 128 - EXPERTS - 2)))
    lo, hi = slice(0, 128), slice(128, 192)
    first = jnp.concatenate([q[:, lo], k[:, lo], v[:, lo], small], axis=0)
    mixed = jnp.concatenate([q[:, hi], k[:, hi]], axis=1)
    last = jnp.concatenate([v[:, hi], o[:, hi]], axis=1)
    second = jnp.concatenate([mixed, o[:, lo], last, small], axis=0)
    return first, second


def unpack(first, second):
    b = [half[i * PART : (i + 1) * PART] for half in (first, second) for i in range(3)]
    q = jnp.concatenate([b[0], b[3][:, :HEAD]], axis=1)
    k = jnp.concatenate([b[1], b[3][:, HEAD:]], axis=1)
    v = jnp.concatenate([b[2], b[5][:, :HEAD]], axis=1)
    o = jnp.concatenate([b[4], b[5][:, HEAD:]], axis=1).T
    small = first[3 * PART : 3 * PART + SMALL]
    gains = small[:, EXPERTS : EXPERTS + 2].T
    return gains[None], jnp.stack([q, k, v], axis=1)[None], o[None], small[None, :, :EXPERTS]


def body(images, cotangent, norm_gains, attn_qkv, attn_out, router, expert_in, expert_out, routes):
    section = lax.axis_index("section")
    core = section.astype(jnp.int32).reshape(1)
    on_first = section == 0

    first, second = pack(norm_gains, attn_qkv, attn_out, router)
    mine = jnp.where(on_first, first, second)
    theirs = swap(jnp.where(on_first, second, first))
    own0 = gather_now(jnp.where(on_first, mine, theirs))
    own1 = gather_later(jnp.where(on_first, theirs, mine))

    w1, w2 = expert_in[0], expert_out[0]
    chosen = jnp.pad(routes[0], ((0, 0), (0, 0), (0, SPAN - SEQ), (0, 126)), constant_values=-1)
    chosen = chosen.reshape(2, PAD, 128)
    own0, w1_other, w2_other, chosen_other = lax.optimization_barrier(
        (own0, swap(w1), swap(w2), swap(chosen))
    )
    routed = (chosen, chosen_other)
    weights = (w1, w1_other, w2, w2_other)
    other0 = swap(own0)

    buf_shape = ((FILL, WIDTH), BF)
    wide_shape = ((FILL, 2 * WIDTH), BF)
    tok_b = ((2, SEQ, WIDTH), BF)
    tok_f = ((2, SEQ, WIDTH), F32)

    buf, *saved0 = whole_call(
        first_kernel, "first", [buf_shape] + SAVED, (core, images, *routed), (own0, other0)
    )
    rows0 = exchange(buf)
    y, q0, gp0 = expert_call(
        expert_forward_kernel, "expert_forward", 0, core, [rows0], weights,
        [(FILL, WIDTH), (FILL, HIDDEN), (FILL, HIDDEN)],
    )
    back = exchange(y)
    own1, _ = lax.optimization_barrier((own1, y))
    other1 = swap(own1)
    h0, c0 = saved0[3], saved0[5]
    x1, y_both, buf, *saved1 = whole_call(
        middle_kernel, "middle", [tok_b, ((PAD, 2 * WIDTH), BF), wide_shape] + SAVED,
        (core, back, h0, c0, *routed, cotangent), (own1, other1),
    )
    rows1 = exchange(buf)
    back, g1_1, g2_1 = expert_call(
        expert_both_kernel, "expert_both", 1, core, [rows1], weights,
        [(FILL, 2 * WIDTH), (WIDTH, HIDDEN), (HIDDEN, WIDTH)],
    )
    to_second, to_first = [(0, 1)], [(1, 0)]
    back, r1_1, r2_1 = lax.optimization_barrier(
        (
            exchange(back),
            lax.ppermute(g1_1, "section", to_second),
            lax.ppermute(g2_1, "section", to_second),
        )
    )
    out_keep, out_send, dx1, ga_keep, ga_send, buf, dgv = whole_call(
        turn_kernel, "turn",
        [tok_b, tok_b, ((PAD, WIDTH), F32), GRADS, GRADS, buf_shape, ((PAD, 128), F32)],
        (core, back, *routed, cotangent, x1, *saved1, y_both, c0), (own1, other1),
    )
    dy0 = exchange(buf)
    partial1 = ga_keep + swap(ga_send)
    partial1, dy0 = lax.optimization_barrier((partial1, dy0))
    rows1_sum = lax.psum_scatter(partial1, "row", scatter_dimension=0, tiled=True)
    back, g1_0, g2_0 = expert_call(
        expert_backward_kernel, "expert_backward", 0, core,
        [rows0, dy0], weights, [(FILL, WIDTH), (WIDTH, HIDDEN), (HIDDEN, WIDTH)], (q0, gp0),
    )
    back, r1_0, r2_0, out_got = lax.optimization_barrier(
        (
            exchange(back),
            lax.ppermute(g1_0, "section", to_first),
            lax.ppermute(g2_0, "section", to_first),
            swap(out_send),
        )
    )
    dx_keep, dx_send, ga_keep, ga_send = whole_call(
        last_kernel, "last", [tok_f, tok_f, GRADS, GRADS],
        (core, back, *routed, dx1, dgv, images, *saved0), (own0, other0),
    )
    g1_0, dx_keep, rows1_sum = lax.optimization_barrier((g1_0, dx_keep, rows1_sum))
    planes1_sum, place = reduce_x(rows1_sum)
    partial0, planes1_sum = lax.optimization_barrier((ga_keep + swap(ga_send), planes1_sum))
    received0 = spread_out(partial0)
    total1 = reduce_step(planes1_sum, place, 1)
    grad_first, grad_second = pair_sum(
        "sum_experts", core, [(g1_0, r1_0, g1_1, r1_1), (g2_0, r2_0, g2_1, r2_1)], F32, 6
    )
    received0, grad_first, grad_second, dx_got = lax.optimization_barrier(
        (received0, grad_first, grad_second, swap(dx_send))
    )
    total0 = add_up(received0)

    def order(kept, got):
        return jnp.where(on_first, kept, got), jnp.where(on_first, got, kept)

    section_out = jnp.stack(order(out_keep, out_got))[None]
    input_grads = jnp.stack(order(dx_keep, dx_got))[None]
    kept, sent = jnp.where(on_first, total0, total1), jnp.where(on_first, total1, total0)
    gains, qkv, out, rout = unpack(*order(kept, swap(sent)))
    return (section_out, input_grads, gains, qkv, out, rout, grad_first[None], grad_second[None])


def solution(mesh):
    in_specs = (
        P(None, ("row", "col"), None, None),
        P(None, ("row", "col"), None, None),
        P("section", None, ("row", "col")),
        P("section", "col", None, "row"),
        P("section", "row", "col"),
        P("section", ("row", "col"), None),
        P("section", None, ("row", "col")),
        P("section", ("row", "col"), None),
        P("section", None, ("row", "col"), None, None),
    )
    out_specs = (
        P("section", None, ("row", "col"), None, None),
        P("section", None, ("row", "col"), None, None),
        P("section", None, ("row", "col")),
        P("section", "col", None, "row"),
        P("section", "row", "col"),
        P("section", ("row", "col"), None),
        P("section", None, ("row", "col")),
        P("section", ("row", "col"), None),
    )
    return jax.shard_map(body, mesh=mesh, in_specs=in_specs, out_specs=out_specs, check_vma=False)
```

```python
import functools

import jax
import jax.numpy as jnp
from jax import lax
from jax.experimental import pallas as pl
from jax.experimental.pallas import tpu as pltpu
from jax.sharding import PartitionSpec as P

HEAD = 64
WIDTH = 768
SEQ = 50
SPAN = 56
PAD = 2 * SPAN
EXPERTS = 32
SLOTS = 8
ROWS = 4
COLS = 16
CHIPS = ROWS * COLS
PART = WIDTH // COLS
SMALL = WIDTH // CHIPS
FILL = CHIPS * SLOTS
HIDDEN = 1536
STEP = 512
EPSILON = 1e-06
SCALE = float(HEAD) ** (-0.5)
VMEM = 58 * 1024 * 1024
BF = jnp.bfloat16
F32 = jnp.float32


def dot(left, right):
    return jnp.dot(left, right, preferred_element_type=F32)


def dot_tn(left, right):
    return lax.dot_general(left, right, (((0,), (0,)), ((), ())), preferred_element_type=F32)


def dot_nt(left, right):
    return lax.dot_general(left, right, (((1,), (1,)), ((), ())), preferred_element_type=F32)


def iota(shape, axis):
    return lax.broadcasted_iota(jnp.int32, shape, axis)


def hot(flag):
    return jnp.where(flag, 1.0, 0.0)


def normalise(values):
    centred = values - jnp.mean(values, axis=-1, keepdims=True)
    spread = jnp.mean(centred * centred, axis=-1, keepdims=True)
    inverse = lax.rsqrt(spread + EPSILON)
    return centred * inverse, inverse


def normalise_back(grad, unit, inverse):
    return inverse * (
        grad
        - jnp.mean(grad, axis=-1, keepdims=True)
        - unit * jnp.mean(grad * unit, axis=-1, keepdims=True)
    )


def gelu_parts(values):
    bell = jnp.exp(-0.5 * values * values)
    t = 1.0 / (1.0 + (0.3275911 * 0.7071067811865476) * jnp.abs(values))
    poly = 1.061405429 * t - 1.453152027
    poly = poly * t + 1.421413741
    poly = poly * t - 0.284496736
    poly = poly * t + 0.254829592
    tail = (0.5 * t) * poly * bell
    below = jnp.where(values < 0, tail, 1.0 - tail)
    return values * below, below + values * (0.3989422804014327 * bell)


def half_turn(values):
    return pltpu.roll(values, HEAD, 1)


def lane_low(rows):
    return iota((rows, 2 * HEAD), 1) < HEAD


def weight_reader(core, own_ref, other_ref, w_ref, small_ref, sems):
    small_copy = pltpu.make_async_copy(own_ref.at[:, 3 * PART : 3 * PART + 16, :], small_ref, sems.at[6, 0])
    small_copy.start()

    def copy(ref, half, r, b):
        at = (3 * half + b) * 128
        return pltpu.make_async_copy(
            ref.at[r * COLS : (r + 1) * COLS, b * PART : (b + 1) * PART, :],
            w_ref.at[r, :, :, at : at + 128],
            sems.at[3 * half + b, r],
        )

    def start(refs):
        for r in range(ROWS):
            for half in range(2):
                for b in range(3):
                    copy(refs[half], half, r, b).start()

    @pl.when(core == 0)
    def _():
        start((own_ref, other_ref))

    @pl.when(core == 1)
    def _():
        start((other_ref, own_ref))

    def wait():
        for r in range(ROWS):
            for half in range(2):
                for b in range(3):
                    copy(own_ref, half, r, b).wait()

    def read(r, first, last):
        return w_ref[r, :, :, first:last].reshape(WIDTH, last - first)

    return small_copy.wait, wait, read


def small_places():
    inside = iota((WIDTH, CHIPS * 16), 1)
    group = lax.shift_right_logical(inside, 4)
    place = jnp.bitwise_and(inside, 15)
    wanted = group * SMALL + place
    return hot((iota((WIDTH, CHIPS * 16), 0) == wanted) & (place < SMALL)).astype(BF)


def unpack_small(small_ref):
    packed = small_ref[...].reshape(CHIPS * 16, 128)
    small = dot(small_places(), packed).astype(BF)
    pick = hot(iota((8, 128), 1) == iota((8, 128), 0) + EXPERTS).astype(BF)
    gains = dot_nt(pick, small)
    return small, gains[0:1], gains[1:2]


def routing(core, section, own_ref, other_ref):
    chosen = jnp.where(core == section, own_ref[core], other_ref[core])
    first = chosen[:, 0:1]
    second = chosen[:, 1:2]
    lane = iota((PAD, 128), 1)
    hot0 = hot(lane == first)
    hot1 = hot(lane == second)
    before = hot(iota((PAD, PAD), 0) > iota((PAD, PAD), 1)).astype(BF)
    earlier = dot(before, (hot0 + hot1).astype(BF))
    place = iota((PAD, FILL), 1)

    def spread(expert, marks):
        slot = jnp.sum(earlier * marks, axis=1, keepdims=True).astype(jnp.int32)
        base = expert * (2 * SLOTS) + slot
        return hot((place == base) | (place == base + SLOTS)).astype(BF)

    return hot0, hot1, spread(first, hot0), spread(second, hot1)


def gates(chance, marks):
    return jnp.sum(chance * marks, axis=1, keepdims=True)


def image_bias():
    query = iota((PAD, PAD), 0)
    key = iota((PAD, PAD), 1)
    first = (query < SPAN) & (key < SEQ)
    second = (query >= SPAN) & (key >= SPAN) & (key < SPAN + SEQ)
    bias = jnp.where(first | second, 0.0, -1e30)
    return jnp.concatenate([bias] * 3, axis=0)


def read_tokens(ref):
    blank = jnp.zeros((SPAN - SEQ, WIDTH), F32)
    return jnp.concatenate([ref[0].astype(F32), blank, ref[1].astype(F32), blank], axis=0)


def write_tokens(ref, values):
    ref[0] = values[:SEQ].astype(ref.dtype)
    ref[1] = values[SPAN : SPAN + SEQ].astype(ref.dtype)


def attention_forward(x, wait, read, gain, m_ref, p_ref, o_ref):
    unit, _ = normalise(x)
    a = (unit * gain).astype(BF)
    low = lane_low(PAD)
    low_b = hot(low).astype(BF)
    high_b = (1.0 - hot(low)).astype(BF)
    bias = image_bias()
    branch = jnp.zeros((PAD, WIDTH), F32)
    wait()
    for r in range(ROWS):
        wide = dot(a, read(r, 0, 512))
        m5 = dot(a, read(r, 640, 768)).astype(BF)
        m = wide.astype(BF)
        m_ref[:, r * 640 : r * 640 + 512] = m
        m_ref[:, r * 640 + 512 : r * 640 + 640] = m5
        q, k, v, qk = m[:, 0:128], m[:, 128:256], m[:, 256:384], m[:, 384:512]
        k2 = half_turn(wide[:, 384:512]).astype(BF)
        qs = jnp.concatenate([q * low_b, q * high_b], axis=0)
        s = jnp.concatenate([dot_nt(qs, k), dot_nt(qk * low_b, k2)], axis=0)
        s = s * SCALE + bias
        e = jnp.exp(s - jnp.max(s, axis=-1, keepdims=True))
        p = (e / jnp.sum(e, axis=-1, keepdims=True)).astype(BF)
        p_ref[r * 3 * PAD : (r + 1) * 3 * PAD, :] = p
        os = dot(p[: 2 * PAD], v)
        o2 = dot(p[2 * PAD :], m5)
        o01 = jnp.where(low, os[:PAD], os[PAD:])
        o2 = jnp.where(low, 0.0, half_turn(o2))
        o = jnp.concatenate([o01, o2], axis=1).astype(BF)
        o_ref[:, r * 256 : (r + 1) * 256] = o
        branch = branch + dot_nt(o, read(r, 512, 768))
    return x + branch


def route_forward(h, small, gain):
    unit, _ = normalise(h)
    b = (unit * gain).astype(BF)
    logits = dot(b, small)
    inside = iota((PAD, 128), 1) < EXPERTS
    logits = jnp.where(inside, logits, -1e30)
    e = jnp.exp(logits - jnp.max(logits, axis=-1, keepdims=True))
    e = jnp.where(inside, e, 0.0)
    return b, e / jnp.sum(e, axis=-1, keepdims=True)


def attention_backward(dh, x, gain, wait, read, m_ref, p_ref, o_ref, take):
    db = dh.astype(BF)
    unit, inverse = normalise(x)
    a = (unit * gain).astype(BF)
    low = lane_low(PAD)
    low_b = hot(low).astype(BF)
    high_b = (1.0 - hot(low)).astype(BF)
    da = jnp.zeros((PAD, WIDTH), F32)
    wait()
    for r in range(ROWS):
        o = o_ref[:, r * 256 : (r + 1) * 256]
        q = m_ref[:, r * 640 : r * 640 + 128]
        k = m_ref[:, r * 640 + 128 : r * 640 + 256]
        v = m_ref[:, r * 640 + 256 : r * 640 + 384]
        qk = m_ref[:, r * 640 + 384 : r * 640 + 512]
        m5 = m_ref[:, r * 640 + 512 : r * 640 + 640]
        k2 = half_turn(qk.astype(F32)).astype(BF)
        q2 = qk * low_b
        qs = jnp.concatenate([q * low_b, q * high_b], axis=0)
        pb = p_ref[r * 3 * PAD : (r + 1) * 3 * PAD, :]
        p = pb.astype(F32)
        do = dot(db, read(r, 512, 768))
        do01 = do[:, 0:128].astype(BF)
        do2 = half_turn(do[:, 128:256]).astype(BF) * low_b
        dos = jnp.concatenate([do01 * low_b, do01 * high_b], axis=0)
        dp = jnp.concatenate([dot_nt(dos, v), dot_nt(do2, m5)], axis=0)
        ds = (p * (dp - jnp.sum(dp * p, axis=-1, keepdims=True))).astype(BF)
        dv = dot_tn(pb[: 2 * PAD], dos)
        dv2 = dot_tn(pb[2 * PAD :], do2)
        dqs = dot(ds[: 2 * PAD], k)
        dq = jnp.where(low, dqs[:PAD], dqs[PAD:]) * SCALE
        dk = dot_tn(ds[: 2 * PAD], qs) * SCALE
        dq2 = dot(ds[2 * PAD :], k2) * SCALE
        dk2 = dot_tn(ds[2 * PAD :], q2) * SCALE
        dqk = jnp.where(low, dq2, half_turn(dk2))
        dm = jnp.concatenate([dq, dk, dv, dqk, dv2], axis=1).astype(BF)
        da = da + dot_nt(dm[:, :512], read(r, 0, 512)) + dot_nt(dm[:, 512:], read(r, 640, 768))
        take(r, a, db, dm)
    dx = dh + normalise_back(da * gain, unit, inverse)
    return dx, a, db, (da * unit).astype(BF)


def projection_grads(r, a, db, dm, o, g_ref):
    gm = dot_tn(a, dm)
    go = dot_tn(db, o)
    blocks = [gm[:, i * 128 : (i + 1) * 128] for i in range(4)]
    blocks += [go[:, :128], gm[:, 512:640] + go[:, 128:256]]
    for i, block in enumerate(blocks):
        at = i % 3 * PART
        g_ref[i // 3, r * COLS : (r + 1) * COLS, at : at + PART, :] = block.astype(BF).reshape(
            COLS, PART, 128
        )


def small_grads(b, dl, terms1, terms2, g_ref):
    lane = iota((PAD, 128), 1)
    gs = dot_tn(b, dl)
    gs = gs + dot_tn(terms1, hot(lane == EXPERTS).astype(BF))
    gs = gs + dot_tn(terms2, hot(lane == EXPERTS + 1).astype(BF))
    spread = dot_tn(small_places(), gs.astype(BF)).astype(BF)
    spread = spread.reshape(CHIPS, 16, 128)
    g_ref[0, :, 3 * PART :, :] = spread
    g_ref[1, :, 3 * PART :, :] = spread


def layer_backward(dz, dr, marks, dgv, x, h, chance, small, gain1, gain2, wait, read, m_ref, p_ref, o_ref, take):
    _, _, d0, d1 = marks
    dn = dot(d0, dr).astype(BF).astype(F32) + dot(d1, dr).astype(BF).astype(F32)
    dl = (chance * (dgv - jnp.sum(dgv * chance, axis=1, keepdims=True))).astype(BF)
    dn = dn + dot_nt(dl, small)
    unit, inverse = normalise(h)
    dh = dz + normalise_back(dn * gain2, unit, inverse)
    dx, a, db, terms1 = attention_backward(dh, x, gain1, wait, read, m_ref, p_ref, o_ref, take)
    return dx, (a, db, dl, terms1, (dn * unit).astype(BF))


def ship(core, g_ref, keep_ref, send_ref, sems):
    copies = send([
        (g_ref.at[1 - core], send_ref, sems.at[0]),
        (g_ref.at[core], keep_ref, sems.at[1]),
    ])
    for copy in copies:
        copy.wait()


def gate_grads(dz, y_both, marks):
    hot0, hot1 = marks[0], marks[1]
    dg0 = jnp.sum(dz * y_both[:, :WIDTH].astype(F32), axis=1, keepdims=True)
    dg1 = jnp.sum(dz * y_both[:, WIDTH:].astype(F32), axis=1, keepdims=True)
    return dg0 * hot0 + dg1 * hot1


def grad_rows(dz, chance, marks):
    hot0, hot1, d0, d1 = marks
    dy0 = (gates(chance, hot0) * dz).astype(BF)
    dy1 = (gates(chance, hot1) * dz).astype(BF)
    return (dot_tn(d0, dy0) + dot_tn(d1, dy1)).astype(BF)


def combine(h, returned, chance, marks):
    hot0, hot1, d0, d1 = marks
    y0 = dot(d0, returned).astype(BF)
    y1 = dot(d1, returned).astype(BF)
    z = h + gates(chance, hot0) * y0.astype(F32) + gates(chance, hot1) * y1.astype(F32)
    return z, jnp.concatenate([y0, y1], axis=1)


def first_kernel(core_ref, x_ref, routes_ref, routes_other_ref, own_ref, other_ref, buf_ref, m_ref, p_ref, o_ref, h_ref, b_ref, c_ref, w_ref, small_ref, w_sems):
    core = core_ref[0]
    ready, wait, read = weight_reader(core, own_ref, other_ref, w_ref, small_ref, w_sems)
    ready()
    small, gain1, gain2 = unpack_small(small_ref)
    marks = routing(core, 0, routes_ref, routes_other_ref)
    h = attention_forward(read_tokens(x_ref.at[core]), wait, read, gain1, m_ref, p_ref, o_ref)
    b, chance = route_forward(h, small, gain2)
    h_ref[...] = h
    b_ref[...] = b
    c_ref[...] = chance
    buf_ref[...] = dot_tn(marks[2] + marks[3], b).astype(BF)


def middle_kernel(core_ref, back_ref, h0_ref, c0_ref, routes_ref, routes_other_ref, cot_ref, own_ref, other_ref, x_ref, y_ref, buf_ref, m_ref, p_ref, o_ref, h_ref, b_ref, c_ref, w_ref, small_ref, w_sems):
    core = core_ref[0]
    ready, wait, read = weight_reader(core, own_ref, other_ref, w_ref, small_ref, w_sems)
    marks = routing(core, 0, routes_ref, routes_other_ref)
    z, y_both = combine(h0_ref[...], back_ref[...], c0_ref[...], marks)
    write_tokens(x_ref, z)
    y_ref[...] = y_both
    ready()
    small, gain1, gain2 = unpack_small(small_ref)
    marks = routing(core, 1, routes_ref, routes_other_ref)
    x = read_tokens(x_ref)
    h = attention_forward(x, wait, read, gain1, m_ref, p_ref, o_ref)
    b, chance = route_forward(h, small, gain2)
    h_ref[...] = h
    b_ref[...] = b
    c_ref[...] = chance
    buf_ref[:, :WIDTH] = dot_tn(marks[2] + marks[3], b).astype(BF)
    buf_ref[:, WIDTH:] = grad_rows(read_tokens(cot_ref.at[core]), chance, marks)


def turn_kernel(core_ref, back_ref, routes_ref, routes_other_ref, cot_ref, x_ref, m_ref, p_ref, o_ref, h_ref, b_ref, c_ref, y0_ref, c0_ref, own_ref, other_ref, keep_ref, send_ref, dx_ref, gk_ref, gs_ref, buf_ref, dgv_ref, w_ref, small_ref, w_sems, g_ref, sems):
    core = core_ref[0]
    ready, wait, read = weight_reader(core, own_ref, other_ref, w_ref, small_ref, w_sems)
    ready()
    small, gain1, gain2 = unpack_small(small_ref)
    marks = routing(core, 1, routes_ref, routes_other_ref)
    chance = c_ref[...]
    h = h_ref[...]
    z, y_both = combine(h, back_ref[:, :WIDTH], chance, marks)
    x = read_tokens(x_ref)
    on_first = core == 0
    write_tokens(keep_ref, jnp.where(on_first, x, z))
    write_tokens(send_ref, jnp.where(on_first, z, x))
    dz = read_tokens(cot_ref.at[core])
    dgv = gate_grads(dz, y_both, marks)

    def take(r, a, db, dm):
        projection_grads(r, a, db, dm, o_ref[:, r * 256 : (r + 1) * 256], g_ref)

    dx, terms = layer_backward(dz, back_ref[:, WIDTH:], marks, dgv, x, h, chance, small, gain1, gain2, wait, read, m_ref, p_ref, o_ref, take)
    dx_ref[...] = dx
    small_grads(b_ref[...], *terms[2:], g_ref)
    dz = dx.astype(BF).astype(F32)
    marks = routing(core, 0, routes_ref, routes_other_ref)
    buf_ref[...] = grad_rows(dz, c0_ref[...], marks)
    dgv_ref[...] = gate_grads(dz, y0_ref[...], marks)
    ship(core, g_ref, gk_ref, gs_ref, sems)


def last_kernel(core_ref, back_ref, routes_ref, routes_other_ref, dz_ref, dgv_ref, x_ref, m_ref, p_ref, o_ref, h_ref, b_ref, c_ref, own_ref, other_ref, keep_ref, send_ref, gk_ref, gs_ref, w_ref, small_ref, w_sems, g_ref, sems):
    core = core_ref[0]
    ready, wait, read = weight_reader(core, own_ref, other_ref, w_ref, small_ref, w_sems)
    ready()
    small, gain1, gain2 = unpack_small(small_ref)
    marks = routing(core, 0, routes_ref, routes_other_ref)
    dx1 = dz_ref[...]
    dz = dx1.astype(BF).astype(F32)

    def take(r, a, db, dm):
        projection_grads(r, a, db, dm, o_ref[:, r * 256 : (r + 1) * 256], g_ref)

    dx, terms = layer_backward(dz, back_ref[...], marks, dgv_ref[...], read_tokens(x_ref.at[core]), h_ref[...], c_ref[...], small, gain1, gain2, wait, read, m_ref, p_ref, o_ref, take)
    small_grads(b_ref[...], *terms[2:], g_ref)
    on_first = core == 0
    write_tokens(keep_ref, jnp.where(on_first, dx, dx1))
    write_tokens(send_ref, jnp.where(on_first, dx1, dx))
    ship(core, g_ref, gk_ref, gs_ref, sems)


def whole_call(kernel, name, outs, args, weights):
    vmem = pl.BlockSpec(memory_space=pltpu.VMEM)
    far = pl.BlockSpec(memory_space=pl.ANY)
    scratch = [
        pltpu.VMEM((ROWS, COLS, PART, WIDTH), BF),
        pltpu.VMEM((CHIPS, 16, 128), BF),
        pltpu.SemaphoreType.DMA((7, ROWS)),
    ]
    if GRADS in outs:
        scratch += [pltpu.VMEM((2,) + GRADS[0], BF), pltpu.SemaphoreType.DMA((2,))]
    return pl.pallas_call(
        kernel,
        name=name,
        out_shape=[jax.ShapeDtypeStruct(shape, dtype) for shape, dtype in outs],
        in_specs=[pl.BlockSpec(memory_space=pltpu.SMEM)] + [vmem] * (len(args) - 1) + [far] * len(weights),
        out_specs=[far if out == GRADS else vmem for out in outs],
        scratch_shapes=scratch,
        compiler_params=pltpu.CompilerParams(vmem_limit_bytes=VMEM),
    )(*args, *weights)


SAVED = [
    ((PAD, ROWS * 640), BF),
    ((ROWS * 3 * PAD, PAD), BF),
    ((PAD, ROWS * 256), BF),
    ((PAD, WIDTH), F32),
    ((PAD, WIDTH), BF),
    ((PAD, 128), F32),
]
GRADS = ((CHIPS, 3 * PART + 16, 128), BF)


def fetch(core, section, own_refs, other_refs, places, sems):
    def start(refs):
        for j in range(HIDDEN // STEP):
            here = slice(j * STEP, (j + 1) * STEP)
            pltpu.make_async_copy(refs[0].at[:, here], places[0].at[:, here], sems.at[0, j]).start()
            pltpu.make_async_copy(refs[1].at[here, :], places[1].at[here, :], sems.at[1, j]).start()

    @pl.when(core == section)
    def _():
        start(own_refs)

    @pl.when(core != section)
    def _():
        start(other_refs)


def fetched(own_refs, places, sems, j):
    here = slice(j * STEP, (j + 1) * STEP)
    pltpu.make_async_copy(own_refs[0].at[:, here], places[0].at[:, here], sems.at[0, j]).wait()
    pltpu.make_async_copy(own_refs[1].at[here, :], places[1].at[here, :], sems.at[1, j]).wait()


def add_to(total, j, value):
    total[...] = value if j == 0 else total[...] + value


def send(pairs):
    copies = [pltpu.make_async_copy(*pair) for pair in pairs]
    for copy in copies:
        copy.start()
    return copies


def expert_forward_kernel(section, core_ref, rows_ref, a_ref, b_ref, c_ref, d_ref, y_ref, q_ref, gp_ref, w1, w2, sems, total, q_s, gp_s, out_sems):
    fetch(core_ref[0], section, (a_ref, c_ref), (b_ref, d_ref), (w1, w2), sems)
    copies = []
    for j in range(HIDDEN // STEP):
        fetched((a_ref, c_ref), (w1, w2), sems, j)
        here = slice(j * STEP, (j + 1) * STEP)
        q, gp = gelu_parts(dot(rows_ref[...], w1[:, here]))
        q = q.astype(BF)
        q_s[:, here] = q
        gp_s[:, here] = gp.astype(BF)
        add_to(total, j, dot(q, w2[here, :]))
        copies += send([
            (q_s.at[:, here], q_ref.at[:, here], out_sems.at[0, j]),
            (gp_s.at[:, here], gp_ref.at[:, here], out_sems.at[1, j]),
        ])
    y_ref[...] = total[...].astype(BF)
    for copy in copies:
        copy.wait()


def expert_both_kernel(section, core_ref, rows_ref, a_ref, b_ref, c_ref, d_ref, back_ref, q_ref, df_ref, w1, w2, sems, total, total_back, q_s, df_s, out_sems):
    fetch(core_ref[0], section, (a_ref, c_ref), (b_ref, d_ref), (w1, w2), sems)
    copies = []
    for j in range(HIDDEN // STEP):
        fetched((a_ref, c_ref), (w1, w2), sems, j)
        here = slice(j * STEP, (j + 1) * STEP)
        q, gp = gelu_parts(dot(rows_ref[:, :WIDTH], w1[:, here]))
        q = q.astype(BF)
        q_s[:, here] = q
        df = (dot_nt(rows_ref[:, WIDTH:], w2[here, :]) * gp).astype(BF)
        df_s[:, here] = df
        add_to(total, j, dot(q, w2[here, :]))
        add_to(total_back, j, dot_nt(df, w1[:, here]))
        copies += send([
            (q_s.at[:, here], q_ref.at[:, here], out_sems.at[0, j]),
            (df_s.at[:, here], df_ref.at[:, here], out_sems.at[1, j]),
        ])
    back_ref[:, :WIDTH] = total[...].astype(BF)
    back_ref[:, WIDTH:] = total_back[...].astype(BF)
    for copy in copies:
        copy.wait()


def expert_backward_kernel(section, core_ref, dy_ref, a_ref, b_ref, c_ref, d_ref, gp_far, back_ref, df_ref, w1, w2, sems, total, df_s, out_sems, gp_ref, in_sems):
    fetch(core_ref[0], section, (a_ref, c_ref), (b_ref, d_ref), (w1, w2), sems)
    kept = []
    for j in range(HIDDEN // STEP):
        here = slice(j * STEP, (j + 1) * STEP)
        kept += send([(gp_far.at[:, here], gp_ref.at[:, here], in_sems.at[0, j])])
    copies = []
    for j in range(HIDDEN // STEP):
        here = slice(j * STEP, (j + 1) * STEP)
        fetched((a_ref, c_ref), (w1, w2), sems, j)
        kept[j].wait()
        df = (dot_nt(dy_ref[...], w2[here, :]) * gp_ref[:, here].astype(F32)).astype(BF)
        df_s[:, here] = df
        add_to(total, j, dot_nt(df, w1[:, here]))
        copies += send([(df_s.at[:, here], df_ref.at[:, here], out_sems.at[0, j])])
    back_ref[...] = total[...].astype(BF)
    for copy in copies:
        copy.wait()


def expert_grads_kernel(rows_ref, dy_ref, q_ref, df_ref, g1_ref, g2_ref, turned):
    @pl.when(pl.program_id(0) == 0)
    def _():
        turned[...] = rows_ref[...].T

    g1_ref[...] = dot(turned[...], df_ref[...]).astype(BF)
    g2_ref[...] = dot_tn(q_ref[...], dy_ref[...]).astype(BF)


def expert_grads(name, rows, dy, dy_at, q, df):
    return pl.pallas_call(
        expert_grads_kernel,
        name=name,
        out_shape=[
            jax.ShapeDtypeStruct((WIDTH, HIDDEN), BF),
            jax.ShapeDtypeStruct((HIDDEN, WIDTH), BF),
        ],
        grid=(HIDDEN // STEP,),
        in_specs=[
            pl.BlockSpec((FILL, WIDTH), lambda i: (0, 0)),
            pl.BlockSpec((FILL, WIDTH), lambda i: (0, dy_at)),
            pl.BlockSpec((FILL, STEP), lambda i: (0, i)),
            pl.BlockSpec((FILL, STEP), lambda i: (0, i)),
        ],
        out_specs=[
            pl.BlockSpec((WIDTH, STEP), lambda i: (0, i)),
            pl.BlockSpec((STEP, WIDTH), lambda i: (i, 0)),
        ],
        scratch_shapes=[pltpu.VMEM((WIDTH, FILL), BF)],
        compiler_params=pltpu.CompilerParams(vmem_limit_bytes=VMEM),
    )(rows, dy, q, df)


def expert_call(kernel, name, section, core, arrays, weights, outs, kept=()):
    vmem = pl.BlockSpec(memory_space=pltpu.VMEM)
    far = pl.BlockSpec(memory_space=pl.ANY)
    rows_f = pltpu.VMEM((FILL, WIDTH), F32)
    hid = pltpu.VMEM((FILL, HIDDEN), BF)
    first, second = pltpu.VMEM((WIDTH, HIDDEN), BF), pltpu.VMEM((HIDDEN, WIDTH), BF)
    sems = pltpu.SemaphoreType.DMA((2, HIDDEN // STEP))
    scratch = {
        "expert_forward": [first, second, sems, rows_f, hid, hid, sems],
        "expert_both": [first, second, sems, rows_f, rows_f, hid, hid, sems],
        "expert_backward": [first, second, sems, rows_f, hid, sems, hid, sems],
    }[name]
    return pl.pallas_call(
        functools.partial(kernel, section),
        name=name,
        out_shape=[jax.ShapeDtypeStruct(shape, BF) for shape in outs],
        in_specs=[pl.BlockSpec(memory_space=pltpu.SMEM)] + [vmem] * len(arrays) + [far] * (4 + len(kept)),
        out_specs=[vmem] + [far] * (len(outs) - 1),
        scratch_shapes=scratch,
        compiler_params=pltpu.CompilerParams(vmem_limit_bytes=VMEM),
    )(core, *arrays, *weights, *kept)


def pair_sum_kernel(count, core_ref, *refs):
    for i in range(count):
        a, b, c, d = refs[4 * i : 4 * i + 4]
        out = refs[4 * count + i]

        @pl.when(core_ref[0] == 0)
        def _(a=a, b=b, out=out):
            out[...] = (a[...].astype(F32) + b[...].astype(F32)).astype(out.dtype)

        @pl.when(core_ref[0] == 1)
        def _(c=c, d=d, out=out):
            out[...] = (c[...].astype(F32) + d[...].astype(F32)).astype(out.dtype)


def pair_sum(name, core, groups, dtype, steps):
    def spec(shape, section):
        block = (shape[0] // steps,) + shape[1:]

        def index(i, core_ref):
            here = i if section is None else jnp.where(core_ref[0] == section, i, 0)
            return (here,) + (0,) * (len(shape) - 1)

        return pl.BlockSpec(block, index)

    return pl.pallas_call(
        functools.partial(pair_sum_kernel, len(groups)),
        name=name,
        out_shape=[jax.ShapeDtypeStruct(group[0].shape, dtype) for group in groups],
        grid_spec=pltpu.PrefetchScalarGridSpec(
            num_scalar_prefetch=1,
            grid=(steps,),
            in_specs=[spec(group[0].shape, section) for group in groups for section in (0, 0, 1, 1)],
            out_specs=[spec(group[0].shape, None) for group in groups],
        ),
        compiler_params=pltpu.CompilerParams(vmem_limit_bytes=VMEM),
    )(core, *[array for group in groups for array in group])


SWAP = [(0, 1), (1, 0)]
CHIP = ("row", "col")


def swap(values):
    return lax.ppermute(values, "section", SWAP)


def exchange(rows):
    wide = rows.shape[1]
    out = lax.all_to_all(
        rows.reshape(CHIPS, SLOTS, wide), CHIP, split_axis=0, concat_axis=0, tiled=True
    )
    return out.reshape(FILL, wide)


def gather_now(chunk):
    copies = jnp.broadcast_to(chunk[None], (CHIPS,) + chunk.shape)
    return lax.all_to_all(copies, CHIP, split_axis=0, concat_axis=0, tiled=True)


def gather_later(chunk):
    return lax.all_gather(chunk, CHIP, axis=0)


def spread_out(partial):
    return lax.all_to_all(partial, CHIP, split_axis=0, concat_axis=0, tiled=True)


def reduce_step(chunks, mine, stride):
    side = 4
    total = lax.dynamic_index_in_dim(chunks, mine, 0, keepdims=False).astype(F32)
    for turn in range(1, side):
        pairs = []
        for at in range(COLS):
            own = at // stride % side
            pairs.append((at, at + ((own + turn) % side - own) * stride))
        chunk = lax.dynamic_index_in_dim(chunks, (mine + turn) % side, 0, keepdims=False)
        total = total + lax.ppermute(chunk, "col", pairs).astype(F32)
    return total


def reduce_x(values):
    place = lax.axis_index("col")
    chunks = values.reshape((4, 4) + values.shape[1:])
    return reduce_step(chunks, place // 4, 4).astype(BF), place % 4


def add_up(received):
    return jnp.sum(received.astype(F32), axis=0)


def pack(norm_gains, attn_qkv, attn_out, router):
    q, k, v = attn_qkv[0, :, 0], attn_qkv[0, :, 1], attn_qkv[0, :, 2]
    o = attn_out[0].T
    small = jnp.concatenate([router[0], norm_gains[0].T], axis=1)
    small = jnp.pad(small, ((0, 16 - SMALL), (0, 128 - EXPERTS - 2)))
    lo, hi = slice(0, 128), slice(128, 192)
    first = jnp.concatenate([q[:, lo], k[:, lo], v[:, lo], small], axis=0)
    mixed = jnp.concatenate([q[:, hi], k[:, hi]], axis=1)
    last = jnp.concatenate([v[:, hi], o[:, hi]], axis=1)
    second = jnp.concatenate([mixed, o[:, lo], last, small], axis=0)
    return first, second


def unpack(first, second):
    b = [half[i * PART : (i + 1) * PART] for half in (first, second) for i in range(3)]
    q = jnp.concatenate([b[0], b[3][:, :HEAD]], axis=1)
    k = jnp.concatenate([b[1], b[3][:, HEAD:]], axis=1)
    v = jnp.concatenate([b[2], b[5][:, :HEAD]], axis=1)
    o = jnp.concatenate([b[4], b[5][:, HEAD:]], axis=1).T
    small = first[3 * PART : 3 * PART + SMALL]
    gains = small[:, EXPERTS : EXPERTS + 2].T
    return gains[None], jnp.stack([q, k, v], axis=1)[None], o[None], small[None, :, :EXPERTS]


def body(images, cotangent, norm_gains, attn_qkv, attn_out, router, expert_in, expert_out, routes):
    section = lax.axis_index("section")
    core = section.astype(jnp.int32).reshape(1)
    on_first = section == 0

    first, second = pack(norm_gains, attn_qkv, attn_out, router)
    mine = jnp.where(on_first, first, second)
    theirs = swap(jnp.where(on_first, second, first))
    own0 = gather_now(jnp.where(on_first, mine, theirs))
    own1 = gather_later(jnp.where(on_first, theirs, mine))

    w1, w2 = expert_in[0], expert_out[0]
    chosen = jnp.pad(routes[0], ((0, 0), (0, 0), (0, SPAN - SEQ), (0, 126)), constant_values=-1)
    chosen = chosen.reshape(2, PAD, 128)
    own0, w1_other, w2_other, chosen_other = lax.optimization_barrier(
        (own0, swap(w1), swap(w2), swap(chosen))
    )
    routed = (chosen, chosen_other)
    weights = (w1, w1_other, w2, w2_other)
    other0 = swap(own0)

    buf_shape = ((FILL, WIDTH), BF)
    wide_shape = ((FILL, 2 * WIDTH), BF)
    tok_b = ((2, SEQ, WIDTH), BF)
    tok_f = ((2, SEQ, WIDTH), F32)

    buf, *saved0 = whole_call(
        first_kernel, "first", [buf_shape] + SAVED, (core, images, *routed), (own0, other0)
    )
    rows0 = exchange(buf)
    y, q0, gp0 = expert_call(
        expert_forward_kernel, "expert_forward", 0, core, [rows0], weights,
        [(FILL, WIDTH), (FILL, HIDDEN), (FILL, HIDDEN)],
    )
    back = exchange(y)
    own1, _ = lax.optimization_barrier((own1, y))
    other1 = swap(own1)
    h0, c0 = saved0[3], saved0[5]
    x1, y_both, buf, *saved1 = whole_call(
        middle_kernel, "middle", [tok_b, ((PAD, 2 * WIDTH), BF), wide_shape] + SAVED,
        (core, back, h0, c0, *routed, cotangent), (own1, other1),
    )
    rows1 = exchange(buf)
    back, q1, df1 = expert_call(
        expert_both_kernel, "expert_both", 1, core, [rows1], weights,
        [(FILL, 2 * WIDTH), (FILL, HIDDEN), (FILL, HIDDEN)],
    )
    g1_1, g2_1 = expert_grads("expert_grads_1", rows1, rows1, 1, q1, df1)
    to_second, to_first = [(0, 1)], [(1, 0)]
    back, g1_1, g2_1 = lax.optimization_barrier((exchange(back), g1_1, g2_1))
    out_keep, out_send, dx1, ga_keep, ga_send, buf, dgv = whole_call(
        turn_kernel, "turn",
        [tok_b, tok_b, ((PAD, WIDTH), F32), GRADS, GRADS, buf_shape, ((PAD, 128), F32)],
        (core, back, *routed, cotangent, x1, *saved1, y_both, c0), (own1, other1),
    )
    dy0 = exchange(buf)
    partial1 = ga_keep + swap(ga_send)
    partial1, dy0, r1_1, r2_1 = lax.optimization_barrier(
        (
            partial1,
            dy0,
            lax.ppermute(g1_1, "section", to_second),
            lax.ppermute(g2_1, "section", to_second),
        )
    )
    rows1_sum = lax.psum_scatter(partial1, "row", scatter_dimension=0, tiled=True)
    back, df0 = expert_call(
        expert_backward_kernel, "expert_backward", 0, core,
        [dy0], weights, [(FILL, WIDTH), (FILL, HIDDEN)], (gp0,),
    )
    g1_0, g2_0 = expert_grads("expert_grads_0", rows0, dy0, 0, q0, df0)
    back, g1_0, g2_0, out_got = lax.optimization_barrier(
        (exchange(back), g1_0, g2_0, swap(out_send))
    )
    r1_0 = lax.ppermute(g1_0, "section", to_first)
    r2_0 = lax.ppermute(g2_0, "section", to_first)
    dx_keep, dx_send, ga_keep, ga_send = whole_call(
        last_kernel, "last", [tok_f, tok_f, GRADS, GRADS],
        (core, back, *routed, dx1, dgv, images, *saved0), (own0, other0),
    )
    g1_0, dx_keep, rows1_sum = lax.optimization_barrier((g1_0, dx_keep, rows1_sum))
    planes1_sum, place = reduce_x(rows1_sum)
    partial0, planes1_sum = lax.optimization_barrier((ga_keep + swap(ga_send), planes1_sum))
    received0 = spread_out(partial0)
    total1 = reduce_step(planes1_sum, place, 1)
    grad_first, grad_second = pair_sum(
        "sum_experts", core, [(g1_0, r1_0, g1_1, r1_1), (g2_0, r2_0, g2_1, r2_1)], F32, 6
    )
    received0, grad_first, grad_second, dx_got = lax.optimization_barrier(
        (received0, grad_first, grad_second, swap(dx_send))
    )
    total0 = add_up(received0)

    def order(kept, got):
        return jnp.where(on_first, kept, got), jnp.where(on_first, got, kept)

    section_out = jnp.stack(order(out_keep, out_got))[None]
    input_grads = jnp.stack(order(dx_keep, dx_got))[None]
    kept, sent = jnp.where(on_first, total0, total1), jnp.where(on_first, total1, total0)
    gains, qkv, out, rout = unpack(*order(kept, swap(sent)))
    return (section_out, input_grads, gains, qkv, out, rout, grad_first[None], grad_second[None])


def solution(mesh):
    in_specs = (
        P(None, ("row", "col"), None, None),
        P(None, ("row", "col"), None, None),
        P("section", None, ("row", "col")),
        P("section", "col", None, "row"),
        P("section", "row", "col"),
        P("section", ("row", "col"), None),
        P("section", None, ("row", "col")),
        P("section", ("row", "col"), None),
        P("section", None, ("row", "col"), None, None),
    )
    out_specs = (
        P("section", None, ("row", "col"), None, None),
        P("section", None, ("row", "col"), None, None),
        P("section", None, ("row", "col")),
        P("section", "col", None, "row"),
        P("section", "row", "col"),
        P("section", ("row", "col"), None),
        P("section", None, ("row", "col")),
        P("section", ("row", "col"), None),
    )
    return jax.shard_map(body, mesh=mesh, in_specs=in_specs, out_specs=out_specs, check_vma=False)
```

```python
import functools

import jax
import jax.numpy as jnp
from jax import lax
from jax.experimental import pallas as pl
from jax.experimental.pallas import tpu as pltpu
from jax.sharding import PartitionSpec as P

HEAD = 64
WIDTH = 768
SEQ = 50
SPAN = 56
PAD = 2 * SPAN
EXPERTS = 32
SLOTS = 8
ROWS = 4
COLS = 16
CHIPS = ROWS * COLS
PART = WIDTH // COLS
SMALL = WIDTH // CHIPS
FILL = CHIPS * SLOTS
HIDDEN = 1536
STEP = 512
EPSILON = 1e-06
SCALE = float(HEAD) ** (-0.5)
VMEM = 58 * 1024 * 1024
BF = jnp.bfloat16
F32 = jnp.float32


def dot(left, right):
    return jnp.dot(left, right, preferred_element_type=F32)


def dot_tn(left, right):
    return lax.dot_general(left, right, (((0,), (0,)), ((), ())), preferred_element_type=F32)


def dot_nt(left, right):
    return lax.dot_general(left, right, (((1,), (1,)), ((), ())), preferred_element_type=F32)


def iota(shape, axis):
    return lax.broadcasted_iota(jnp.int32, shape, axis)


def hot(flag):
    return jnp.where(flag, 1.0, 0.0)


def normalise(values):
    centred = values - jnp.mean(values, axis=-1, keepdims=True)
    spread = jnp.mean(centred * centred, axis=-1, keepdims=True)
    inverse = lax.rsqrt(spread + EPSILON)
    return centred * inverse, inverse


def normalise_back(grad, unit, inverse):
    return inverse * (
        grad
        - jnp.mean(grad, axis=-1, keepdims=True)
        - unit * jnp.mean(grad * unit, axis=-1, keepdims=True)
    )


def gelu_parts(values):
    bell = jnp.exp(-0.5 * values * values)
    t = 1.0 / (1.0 + (0.3275911 * 0.7071067811865476) * jnp.abs(values))
    poly = 1.061405429 * t - 1.453152027
    poly = poly * t + 1.421413741
    poly = poly * t - 0.284496736
    poly = poly * t + 0.254829592
    tail = (0.5 * t) * poly * bell
    below = jnp.where(values < 0, tail, 1.0 - tail)
    return values * below, below + values * (0.3989422804014327 * bell)


def half_turn(values):
    return pltpu.roll(values, HEAD, 1)


def lane_low(rows):
    return iota((rows, 2 * HEAD), 1) < HEAD


def weight_reader(core, own_ref, other_ref, w_ref, small_ref, sems):
    small_copy = pltpu.make_async_copy(own_ref.at[:, 3 * PART : 3 * PART + 16, :], small_ref, sems.at[6, 0])
    small_copy.start()

    def copy(ref, half, r, b):
        at = (3 * half + b) * 128
        return pltpu.make_async_copy(
            ref.at[r * COLS : (r + 1) * COLS, b * PART : (b + 1) * PART, :],
            w_ref.at[r, :, :, at : at + 128],
            sems.at[3 * half + b, r],
        )

    def start(refs):
        for r in range(ROWS):
            for half in range(2):
                for b in range(3):
                    copy(refs[half], half, r, b).start()

    @pl.when(core == 0)
    def _():
        start((own_ref, other_ref))

    @pl.when(core == 1)
    def _():
        start((other_ref, own_ref))

    def wait():
        for r in range(ROWS):
            for half in range(2):
                for b in range(3):
                    copy(own_ref, half, r, b).wait()

    def read(r, first, last):
        return w_ref[r, :, :, first:last].reshape(WIDTH, last - first)

    return small_copy.wait, wait, read


def small_places():
    shape = (COLS * SMALL, COLS * 16)
    inside = iota(shape, 1)
    place = jnp.bitwise_and(inside, 15)
    wanted = lax.shift_right_logical(inside, 4) * SMALL + place
    return hot((iota(shape, 0) == wanted) & (place < SMALL)).astype(BF)


def unpack_small(small_ref):
    packed = small_ref[...].reshape(ROWS, COLS * 16, 128)
    places = small_places()
    small = jnp.concatenate([dot(places, packed[r]) for r in range(ROWS)], axis=0).astype(BF)
    pick = hot(iota((8, 128), 1) == iota((8, 128), 0) + EXPERTS).astype(BF)
    gains = dot_nt(pick, small)
    return small, gains[0:1], gains[1:2]


def routing(core, section, own_ref, other_ref):
    chosen = jnp.where(core == section, own_ref[core], other_ref[core])
    first = chosen[:, 0:1]
    second = chosen[:, 1:2]
    lane = iota((PAD, 128), 1)
    hot0 = hot(lane == first)
    hot1 = hot(lane == second)
    before = hot(iota((PAD, PAD), 0) > iota((PAD, PAD), 1)).astype(BF)
    earlier = dot(before, (hot0 + hot1).astype(BF))
    place = iota((PAD, FILL), 1)

    def spread(expert, marks):
        slot = jnp.sum(earlier * marks, axis=1, keepdims=True).astype(jnp.int32)
        base = expert * (2 * SLOTS) + slot
        return hot((place == base) | (place == base + SLOTS)).astype(BF)

    return hot0, hot1, spread(first, hot0), spread(second, hot1)


def gates(chance, marks):
    return jnp.sum(chance * marks, axis=1, keepdims=True)


def image_bias():
    query = iota((PAD, PAD), 0)
    key = iota((PAD, PAD), 1)
    first = (query < SPAN) & (key < SEQ)
    second = (query >= SPAN) & (key >= SPAN) & (key < SPAN + SEQ)
    bias = jnp.where(first | second, 0.0, -1e30)
    return jnp.concatenate([bias] * 3, axis=0)


def read_tokens(ref):
    blank = jnp.zeros((SPAN - SEQ, WIDTH), F32)
    return jnp.concatenate([ref[0].astype(F32), blank, ref[1].astype(F32), blank], axis=0)


def write_tokens(ref, values):
    ref[0] = values[:SEQ].astype(ref.dtype)
    ref[1] = values[SPAN : SPAN + SEQ].astype(ref.dtype)


def attention_forward(x, wait, read, gain, m_ref, p_ref, o_ref):
    unit, _ = normalise(x)
    a = (unit * gain).astype(BF)
    low = lane_low(PAD)
    low_b = hot(low).astype(BF)
    high_b = (1.0 - hot(low)).astype(BF)
    bias = image_bias()
    branch = jnp.zeros((PAD, WIDTH), F32)
    wait()
    for r in range(ROWS):
        wide = dot(a, read(r, 0, 512))
        m5 = dot(a, read(r, 640, 768)).astype(BF)
        m = wide.astype(BF)
        m_ref[:, r * 640 : r * 640 + 512] = m
        m_ref[:, r * 640 + 512 : r * 640 + 640] = m5
        q, k, v, qk = m[:, 0:128], m[:, 128:256], m[:, 256:384], m[:, 384:512]
        k2 = half_turn(wide[:, 384:512]).astype(BF)
        qs = jnp.concatenate([q * low_b, q * high_b], axis=0)
        s = jnp.concatenate([dot_nt(qs, k), dot_nt(qk * low_b, k2)], axis=0)
        s = s * SCALE + bias
        e = jnp.exp(s - jnp.max(s, axis=-1, keepdims=True))
        p = (e / jnp.sum(e, axis=-1, keepdims=True)).astype(BF)
        p_ref[r * 3 * PAD : (r + 1) * 3 * PAD, :] = p
        os = dot(p[: 2 * PAD], v)
        o2 = dot(p[2 * PAD :], m5)
        o01 = jnp.where(low, os[:PAD], os[PAD:])
        o2 = jnp.where(low, 0.0, half_turn(o2))
        o = jnp.concatenate([o01, o2], axis=1).astype(BF)
        o_ref[:, r * 256 : (r + 1) * 256] = o
        branch = branch + dot_nt(o, read(r, 512, 768))
    return x + branch


def route_forward(h, small, gain):
    unit, _ = normalise(h)
    b = (unit * gain).astype(BF)
    logits = dot(b, small)
    inside = iota((PAD, 128), 1) < EXPERTS
    logits = jnp.where(inside, logits, -1e30)
    e = jnp.exp(logits - jnp.max(logits, axis=-1, keepdims=True))
    e = jnp.where(inside, e, 0.0)
    return b, e / jnp.sum(e, axis=-1, keepdims=True)


def attention_backward(dh, x, gain, wait, read, m_ref, p_ref, o_ref, take):
    db = dh.astype(BF)
    unit, inverse = normalise(x)
    a = (unit * gain).astype(BF)
    low = lane_low(PAD)
    low_b = hot(low).astype(BF)
    high_b = (1.0 - hot(low)).astype(BF)
    da = jnp.zeros((PAD, WIDTH), F32)
    wait()
    for r in range(ROWS):
        o = o_ref[:, r * 256 : (r + 1) * 256]
        q = m_ref[:, r * 640 : r * 640 + 128]
        k = m_ref[:, r * 640 + 128 : r * 640 + 256]
        v = m_ref[:, r * 640 + 256 : r * 640 + 384]
        qk = m_ref[:, r * 640 + 384 : r * 640 + 512]
        m5 = m_ref[:, r * 640 + 512 : r * 640 + 640]
        k2 = half_turn(qk.astype(F32)).astype(BF)
        q2 = qk * low_b
        qs = jnp.concatenate([q * low_b, q * high_b], axis=0)
        pb = p_ref[r * 3 * PAD : (r + 1) * 3 * PAD, :]
        p = pb.astype(F32)
        do = dot(db, read(r, 512, 768))
        do01 = do[:, 0:128].astype(BF)
        do2 = half_turn(do[:, 128:256]).astype(BF) * low_b
        dos = jnp.concatenate([do01 * low_b, do01 * high_b], axis=0)
        dp = jnp.concatenate([dot_nt(dos, v), dot_nt(do2, m5)], axis=0)
        ds = (p * (dp - jnp.sum(dp * p, axis=-1, keepdims=True))).astype(BF)
        dv = dot_tn(pb[: 2 * PAD], dos)
        dv2 = dot_tn(pb[2 * PAD :], do2)
        dqs = dot(ds[: 2 * PAD], k)
        dq = jnp.where(low, dqs[:PAD], dqs[PAD:]) * SCALE
        dk = dot_tn(ds[: 2 * PAD], qs) * SCALE
        dq2 = dot(ds[2 * PAD :], k2) * SCALE
        dk2 = dot_tn(ds[2 * PAD :], q2) * SCALE
        dqk = jnp.where(low, dq2, half_turn(dk2))
        dm = jnp.concatenate([dq, dk, dv, dqk, dv2], axis=1).astype(BF)
        da = da + dot_nt(dm[:, :512], read(r, 0, 512)) + dot_nt(dm[:, 512:], read(r, 640, 768))
        take(r, a, db, dm)
    dx = dh + normalise_back(da * gain, unit, inverse)
    return dx, a, db, (da * unit).astype(BF)


def projection_grads(r, a, db, dm, o, g_ref):
    gm = dot_tn(a, dm)
    go = dot_tn(db, o)
    blocks = [gm[:, i * 128 : (i + 1) * 128] for i in range(4)]
    blocks += [go[:, :128], gm[:, 512:640] + go[:, 128:256]]
    for i, block in enumerate(blocks):
        at = i % 3 * PART
        g_ref[i // 3, r * COLS : (r + 1) * COLS, at : at + PART, :] = block.astype(BF).reshape(
            COLS, PART, 128
        )


def small_grads(b, dl, terms1, terms2, g_ref):
    lane = iota((PAD, 128), 1)
    gs = dot_tn(b, dl)
    gs = gs + dot_tn(terms1, hot(lane == EXPERTS).astype(BF))
    gs = gs + dot_tn(terms2, hot(lane == EXPERTS + 1).astype(BF))
    gs = gs.astype(BF).reshape(ROWS, COLS * SMALL, 128)
    places = small_places()
    spread = jnp.concatenate([dot_tn(places, gs[r]) for r in range(ROWS)], axis=0).astype(BF)
    spread = spread.reshape(CHIPS, 16, 128)
    g_ref[0, :, 3 * PART :, :] = spread
    g_ref[1, :, 3 * PART :, :] = spread


def layer_backward(dz, dr, marks, dgv, x, h, chance, small, gain1, gain2, wait, read, m_ref, p_ref, o_ref, take):
    _, _, d0, d1 = marks
    dn = dot(d0, dr).astype(BF).astype(F32) + dot(d1, dr).astype(BF).astype(F32)
    dl = (chance * (dgv - jnp.sum(dgv * chance, axis=1, keepdims=True))).astype(BF)
    dn = dn + dot_nt(dl, small)
    unit, inverse = normalise(h)
    dh = dz + normalise_back(dn * gain2, unit, inverse)
    dx, a, db, terms1 = attention_backward(dh, x, gain1, wait, read, m_ref, p_ref, o_ref, take)
    return dx, (a, db, dl, terms1, (dn * unit).astype(BF))


def ship(core, g_ref, keep_ref, send_ref, sems):
    copies = send([
        (g_ref.at[1 - core], send_ref, sems.at[0]),
        (g_ref.at[core], keep_ref, sems.at[1]),
    ])
    for copy in copies:
        copy.wait()


def gate_grads(dz, y_both, marks):
    hot0, hot1 = marks[0], marks[1]
    dg0 = jnp.sum(dz * y_both[:, :WIDTH].astype(F32), axis=1, keepdims=True)
    dg1 = jnp.sum(dz * y_both[:, WIDTH:].astype(F32), axis=1, keepdims=True)
    return dg0 * hot0 + dg1 * hot1


def grad_rows(dz, chance, marks):
    hot0, hot1, d0, d1 = marks
    dy0 = (gates(chance, hot0) * dz).astype(BF)
    dy1 = (gates(chance, hot1) * dz).astype(BF)
    return (dot_tn(d0, dy0) + dot_tn(d1, dy1)).astype(BF)


def combine(h, returned, chance, marks):
    hot0, hot1, d0, d1 = marks
    y0 = dot(d0, returned).astype(BF)
    y1 = dot(d1, returned).astype(BF)
    z = h + gates(chance, hot0) * y0.astype(F32) + gates(chance, hot1) * y1.astype(F32)
    return z, jnp.concatenate([y0, y1], axis=1)


def first_kernel(core_ref, x_ref, routes_ref, routes_other_ref, own_ref, other_ref, buf_ref, m_ref, p_ref, o_ref, h_ref, b_ref, c_ref, w_ref, small_ref, w_sems):
    core = core_ref[0]
    ready, wait, read = weight_reader(core, own_ref, other_ref, w_ref, small_ref, w_sems)
    ready()
    small, gain1, gain2 = unpack_small(small_ref)
    marks = routing(core, 0, routes_ref, routes_other_ref)
    h = attention_forward(read_tokens(x_ref.at[core]), wait, read, gain1, m_ref, p_ref, o_ref)
    b, chance = route_forward(h, small, gain2)
    h_ref[...] = h
    b_ref[...] = b
    c_ref[...] = chance
    buf_ref[...] = dot_tn(marks[2] + marks[3], b).astype(BF)


def middle_kernel(core_ref, back_ref, h0_ref, c0_ref, routes_ref, routes_other_ref, cot_ref, own_ref, other_ref, x_ref, y_ref, buf_ref, m_ref, p_ref, o_ref, h_ref, b_ref, c_ref, w_ref, small_ref, w_sems):
    core = core_ref[0]
    ready, wait, read = weight_reader(core, own_ref, other_ref, w_ref, small_ref, w_sems)
    marks = routing(core, 0, routes_ref, routes_other_ref)
    z, y_both = combine(h0_ref[...], back_ref[...], c0_ref[...], marks)
    write_tokens(x_ref, z)
    y_ref[...] = y_both
    ready()
    small, gain1, gain2 = unpack_small(small_ref)
    marks = routing(core, 1, routes_ref, routes_other_ref)
    x = read_tokens(x_ref)
    h = attention_forward(x, wait, read, gain1, m_ref, p_ref, o_ref)
    b, chance = route_forward(h, small, gain2)
    h_ref[...] = h
    b_ref[...] = b
    c_ref[...] = chance
    buf_ref[:, :WIDTH] = dot_tn(marks[2] + marks[3], b).astype(BF)
    buf_ref[:, WIDTH:] = grad_rows(read_tokens(cot_ref.at[core]), chance, marks)


def turn_kernel(core_ref, back_ref, routes_ref, routes_other_ref, cot_ref, x_ref, m_ref, p_ref, o_ref, h_ref, b_ref, c_ref, y0_ref, c0_ref, own_ref, other_ref, keep_ref, send_ref, dx_ref, gk_ref, gs_ref, buf_ref, dgv_ref, w_ref, small_ref, w_sems, g_ref, sems):
    core = core_ref[0]
    ready, wait, read = weight_reader(core, own_ref, other_ref, w_ref, small_ref, w_sems)
    ready()
    small, gain1, gain2 = unpack_small(small_ref)
    marks = routing(core, 1, routes_ref, routes_other_ref)
    chance = c_ref[...]
    h = h_ref[...]
    z, y_both = combine(h, back_ref[:, :WIDTH], chance, marks)
    x = read_tokens(x_ref)
    on_first = core == 0
    write_tokens(keep_ref, jnp.where(on_first, x, z))
    write_tokens(send_ref, jnp.where(on_first, z, x))
    dz = read_tokens(cot_ref.at[core])
    dgv = gate_grads(dz, y_both, marks)

    def take(r, a, db, dm):
        projection_grads(r, a, db, dm, o_ref[:, r * 256 : (r + 1) * 256], g_ref)

    dx, terms = layer_backward(dz, back_ref[:, WIDTH:], marks, dgv, x, h, chance, small, gain1, gain2, wait, read, m_ref, p_ref, o_ref, take)
    dx_ref[...] = dx
    small_grads(b_ref[...], *terms[2:], g_ref)
    dz = dx.astype(BF).astype(F32)
    marks = routing(core, 0, routes_ref, routes_other_ref)
    buf_ref[...] = grad_rows(dz, c0_ref[...], marks)
    dgv_ref[...] = gate_grads(dz, y0_ref[...], marks)
    ship(core, g_ref, gk_ref, gs_ref, sems)


def last_kernel(core_ref, back_ref, routes_ref, routes_other_ref, dz_ref, dgv_ref, x_ref, m_ref, p_ref, o_ref, h_ref, b_ref, c_ref, own_ref, other_ref, keep_ref, send_ref, gk_ref, gs_ref, w_ref, small_ref, w_sems, g_ref, sems):
    core = core_ref[0]
    ready, wait, read = weight_reader(core, own_ref, other_ref, w_ref, small_ref, w_sems)
    ready()
    small, gain1, gain2 = unpack_small(small_ref)
    marks = routing(core, 0, routes_ref, routes_other_ref)
    dx1 = dz_ref[...]
    dz = dx1.astype(BF).astype(F32)

    def take(r, a, db, dm):
        projection_grads(r, a, db, dm, o_ref[:, r * 256 : (r + 1) * 256], g_ref)

    dx, terms = layer_backward(dz, back_ref[...], marks, dgv_ref[...], read_tokens(x_ref.at[core]), h_ref[...], c_ref[...], small, gain1, gain2, wait, read, m_ref, p_ref, o_ref, take)
    small_grads(b_ref[...], *terms[2:], g_ref)
    on_first = core == 0
    write_tokens(keep_ref, jnp.where(on_first, dx, dx1))
    write_tokens(send_ref, jnp.where(on_first, dx1, dx))
    ship(core, g_ref, gk_ref, gs_ref, sems)


def whole_call(kernel, name, outs, args, weights):
    vmem = pl.BlockSpec(memory_space=pltpu.VMEM)
    far = pl.BlockSpec(memory_space=pl.ANY)
    scratch = [
        pltpu.VMEM((ROWS, COLS, PART, WIDTH), BF),
        pltpu.VMEM((CHIPS, 16, 128), BF),
        pltpu.SemaphoreType.DMA((7, ROWS)),
    ]
    if GRADS in outs:
        scratch += [pltpu.VMEM((2,) + GRADS[0], BF), pltpu.SemaphoreType.DMA((2,))]
    return pl.pallas_call(
        kernel,
        name=name,
        out_shape=[jax.ShapeDtypeStruct(shape, dtype) for shape, dtype in outs],
        in_specs=[pl.BlockSpec(memory_space=pltpu.SMEM)] + [vmem] * (len(args) - 1) + [far] * len(weights),
        out_specs=[far if out == GRADS else vmem for out in outs],
        scratch_shapes=scratch,
        compiler_params=pltpu.CompilerParams(vmem_limit_bytes=VMEM),
    )(*args, *weights)


SAVED = [
    ((PAD, ROWS * 640), BF),
    ((ROWS * 3 * PAD, PAD), BF),
    ((PAD, ROWS * 256), BF),
    ((PAD, WIDTH), F32),
    ((PAD, WIDTH), BF),
    ((PAD, 128), F32),
]
GRADS = ((CHIPS, 3 * PART + 16, 128), BF)


def fetch(core, section, own_refs, other_refs, places, sems):
    def start(refs):
        for j in range(HIDDEN // STEP):
            here = slice(j * STEP, (j + 1) * STEP)
            pltpu.make_async_copy(refs[0].at[:, here], places[0].at[:, here], sems.at[0, j]).start()
            pltpu.make_async_copy(refs[1].at[here, :], places[1].at[here, :], sems.at[1, j]).start()

    @pl.when(core == section)
    def _():
        start(own_refs)

    @pl.when(core != section)
    def _():
        start(other_refs)


def fetched(own_refs, places, sems, j):
    here = slice(j * STEP, (j + 1) * STEP)
    pltpu.make_async_copy(own_refs[0].at[:, here], places[0].at[:, here], sems.at[0, j]).wait()
    pltpu.make_async_copy(own_refs[1].at[here, :], places[1].at[here, :], sems.at[1, j]).wait()


def add_to(total, j, value):
    total[...] = value if j == 0 else total[...] + value


def send(pairs):
    copies = [pltpu.make_async_copy(*pair) for pair in pairs]
    for copy in copies:
        copy.start()
    return copies


def expert_forward_kernel(section, core_ref, rows_ref, a_ref, b_ref, c_ref, d_ref, y_ref, q_ref, gp_ref, w1, w2, sems, total, q_s, gp_s, out_sems):
    fetch(core_ref[0], section, (a_ref, c_ref), (b_ref, d_ref), (w1, w2), sems)
    copies = []
    for j in range(HIDDEN // STEP):
        fetched((a_ref, c_ref), (w1, w2), sems, j)
        here = slice(j * STEP, (j + 1) * STEP)
        q, gp = gelu_parts(dot(rows_ref[...], w1[:, here]))
        q = q.astype(BF)
        q_s[:, here] = q
        gp_s[:, here] = gp.astype(BF)
        add_to(total, j, dot(q, w2[here, :]))
        copies += send([
            (q_s.at[:, here], q_ref.at[:, here], out_sems.at[0, j]),
            (gp_s.at[:, here], gp_ref.at[:, here], out_sems.at[1, j]),
        ])
    y_ref[...] = total[...].astype(BF)
    for copy in copies:
        copy.wait()


def expert_both_kernel(section, core_ref, rows_ref, a_ref, b_ref, c_ref, d_ref, back_ref, q_ref, df_ref, w1, w2, sems, total, total_back, q_s, df_s, out_sems):
    fetch(core_ref[0], section, (a_ref, c_ref), (b_ref, d_ref), (w1, w2), sems)
    copies = []
    for j in range(HIDDEN // STEP):
        fetched((a_ref, c_ref), (w1, w2), sems, j)
        here = slice(j * STEP, (j + 1) * STEP)
        q, gp = gelu_parts(dot(rows_ref[:, :WIDTH], w1[:, here]))
        q = q.astype(BF)
        q_s[:, here] = q
        df = (dot_nt(rows_ref[:, WIDTH:], w2[here, :]) * gp).astype(BF)
        df_s[:, here] = df
        add_to(total, j, dot(q, w2[here, :]))
        add_to(total_back, j, dot_nt(df, w1[:, here]))
        copies += send([
            (q_s.at[:, here], q_ref.at[:, here], out_sems.at[0, j]),
            (df_s.at[:, here], df_ref.at[:, here], out_sems.at[1, j]),
        ])
    back_ref[:, :WIDTH] = total[...].astype(BF)
    back_ref[:, WIDTH:] = total_back[...].astype(BF)
    for copy in copies:
        copy.wait()


def expert_backward_kernel(section, core_ref, dy_ref, a_ref, b_ref, c_ref, d_ref, gp_far, back_ref, df_ref, w1, w2, sems, total, df_s, out_sems, gp_ref, in_sems):
    fetch(core_ref[0], section, (a_ref, c_ref), (b_ref, d_ref), (w1, w2), sems)
    kept = []
    for j in range(HIDDEN // STEP):
        here = slice(j * STEP, (j + 1) * STEP)
        kept += send([(gp_far.at[:, here], gp_ref.at[:, here], in_sems.at[0, j])])
    copies = []
    for j in range(HIDDEN // STEP):
        here = slice(j * STEP, (j + 1) * STEP)
        fetched((a_ref, c_ref), (w1, w2), sems, j)
        kept[j].wait()
        df = (dot_nt(dy_ref[...], w2[here, :]) * gp_ref[:, here].astype(F32)).astype(BF)
        df_s[:, here] = df
        add_to(total, j, dot_nt(df, w1[:, here]))
        copies += send([(df_s.at[:, here], df_ref.at[:, here], out_sems.at[0, j])])
    back_ref[...] = total[...].astype(BF)
    for copy in copies:
        copy.wait()


def expert_grads_kernel(rows_ref, dy_ref, q_ref, df_ref, g1_ref, g2_ref, turned):
    @pl.when(pl.program_id(0) == 0)
    def _():
        turned[...] = rows_ref[...].T

    g1_ref[...] = dot(turned[...], df_ref[...]).astype(BF)
    g2_ref[...] = dot_tn(q_ref[...], dy_ref[...]).astype(BF)


def expert_grads(name, rows, dy, dy_at, q, df):
    return pl.pallas_call(
        expert_grads_kernel,
        name=name,
        out_shape=[
            jax.ShapeDtypeStruct((WIDTH, HIDDEN), BF),
            jax.ShapeDtypeStruct((HIDDEN, WIDTH), BF),
        ],
        grid=(HIDDEN // STEP,),
        in_specs=[
            pl.BlockSpec((FILL, WIDTH), lambda i: (0, 0)),
            pl.BlockSpec((FILL, WIDTH), lambda i: (0, dy_at)),
            pl.BlockSpec((FILL, STEP), lambda i: (0, i)),
            pl.BlockSpec((FILL, STEP), lambda i: (0, i)),
        ],
        out_specs=[
            pl.BlockSpec((WIDTH, STEP), lambda i: (0, i)),
            pl.BlockSpec((STEP, WIDTH), lambda i: (i, 0)),
        ],
        scratch_shapes=[pltpu.VMEM((WIDTH, FILL), BF)],
        compiler_params=pltpu.CompilerParams(vmem_limit_bytes=VMEM),
    )(rows, dy, q, df)


def expert_call(kernel, name, section, core, arrays, weights, outs, kept=()):
    vmem = pl.BlockSpec(memory_space=pltpu.VMEM)
    far = pl.BlockSpec(memory_space=pl.ANY)
    rows_f = pltpu.VMEM((FILL, WIDTH), F32)
    hid = pltpu.VMEM((FILL, HIDDEN), BF)
    first, second = pltpu.VMEM((WIDTH, HIDDEN), BF), pltpu.VMEM((HIDDEN, WIDTH), BF)
    sems = pltpu.SemaphoreType.DMA((2, HIDDEN // STEP))
    scratch = {
        "expert_forward": [first, second, sems, rows_f, hid, hid, sems],
        "expert_both": [first, second, sems, rows_f, rows_f, hid, hid, sems],
        "expert_backward": [first, second, sems, rows_f, hid, sems, hid, sems],
    }[name]
    return pl.pallas_call(
        functools.partial(kernel, section),
        name=name,
        out_shape=[jax.ShapeDtypeStruct(shape, BF) for shape in outs],
        in_specs=[pl.BlockSpec(memory_space=pltpu.SMEM)] + [vmem] * len(arrays) + [far] * (4 + len(kept)),
        out_specs=[vmem] + [far] * (len(outs) - 1),
        scratch_shapes=scratch,
        compiler_params=pltpu.CompilerParams(vmem_limit_bytes=VMEM),
    )(core, *arrays, *weights, *kept)


def pair_sum_kernel(count, core_ref, *refs):
    for i in range(count):
        a, b, c, d = refs[4 * i : 4 * i + 4]
        out = refs[4 * count + i]

        @pl.when(core_ref[0] == 0)
        def _(a=a, b=b, out=out):
            out[...] = (a[...].astype(F32) + b[...].astype(F32)).astype(out.dtype)

        @pl.when(core_ref[0] == 1)
        def _(c=c, d=d, out=out):
            out[...] = (c[...].astype(F32) + d[...].astype(F32)).astype(out.dtype)


def pair_sum(name, core, groups, dtype, steps):
    def spec(shape, section):
        block = (shape[0] // steps,) + shape[1:]

        def index(i, core_ref):
            here = i if section is None else jnp.where(core_ref[0] == section, i, 0)
            return (here,) + (0,) * (len(shape) - 1)

        return pl.BlockSpec(block, index)

    return pl.pallas_call(
        functools.partial(pair_sum_kernel, len(groups)),
        name=name,
        out_shape=[jax.ShapeDtypeStruct(group[0].shape, dtype) for group in groups],
        grid_spec=pltpu.PrefetchScalarGridSpec(
            num_scalar_prefetch=1,
            grid=(steps,),
            in_specs=[spec(group[0].shape, section) for group in groups for section in (0, 0, 1, 1)],
            out_specs=[spec(group[0].shape, None) for group in groups],
        ),
        compiler_params=pltpu.CompilerParams(vmem_limit_bytes=VMEM),
    )(core, *[array for group in groups for array in group])


SWAP = [(0, 1), (1, 0)]
CHIP = ("row", "col")


def swap(values):
    return lax.ppermute(values, "section", SWAP)


def exchange(rows):
    wide = rows.shape[1]
    out = lax.all_to_all(
        rows.reshape(CHIPS, SLOTS, wide), CHIP, split_axis=0, concat_axis=0, tiled=True
    )
    return out.reshape(FILL, wide)


def gather_now(chunk):
    copies = jnp.broadcast_to(chunk[None], (CHIPS,) + chunk.shape)
    return lax.all_to_all(copies, CHIP, split_axis=0, concat_axis=0, tiled=True)


def gather_later(chunk):
    return lax.all_gather(chunk, CHIP, axis=0)


def spread_out(partial):
    return lax.all_to_all(partial, CHIP, split_axis=0, concat_axis=0, tiled=True)


def reduce_step(chunks, mine, stride):
    side = 4
    total = lax.dynamic_index_in_dim(chunks, mine, 0, keepdims=False).astype(F32)
    for turn in range(1, side):
        pairs = []
        for at in range(COLS):
            own = at // stride % side
            pairs.append((at, at + ((own + turn) % side - own) * stride))
        chunk = lax.dynamic_index_in_dim(chunks, (mine + turn) % side, 0, keepdims=False)
        total = total + lax.ppermute(chunk, "col", pairs).astype(F32)
    return total


def reduce_x(values):
    place = lax.axis_index("col")
    chunks = values.reshape((4, 4) + values.shape[1:])
    return reduce_step(chunks, place // 4, 4).astype(BF), place % 4


def add_up(received):
    return jnp.sum(received.astype(F32), axis=0)


def pack(norm_gains, attn_qkv, attn_out, router):
    q, k, v = attn_qkv[0, :, 0], attn_qkv[0, :, 1], attn_qkv[0, :, 2]
    o = attn_out[0].T
    small = jnp.concatenate([router[0], norm_gains[0].T], axis=1)
    small = jnp.pad(small, ((0, 16 - SMALL), (0, 128 - EXPERTS - 2)))
    lo, hi = slice(0, 128), slice(128, 192)
    first = jnp.concatenate([q[:, lo], k[:, lo], v[:, lo], small], axis=0)
    mixed = jnp.concatenate([q[:, hi], k[:, hi]], axis=1)
    last = jnp.concatenate([v[:, hi], o[:, hi]], axis=1)
    second = jnp.concatenate([mixed, o[:, lo], last, small], axis=0)
    return first, second


def unpack(first, second):
    b = [half[i * PART : (i + 1) * PART] for half in (first, second) for i in range(3)]
    q = jnp.concatenate([b[0], b[3][:, :HEAD]], axis=1)
    k = jnp.concatenate([b[1], b[3][:, HEAD:]], axis=1)
    v = jnp.concatenate([b[2], b[5][:, :HEAD]], axis=1)
    o = jnp.concatenate([b[4], b[5][:, HEAD:]], axis=1).T
    small = first[3 * PART : 3 * PART + SMALL]
    gains = small[:, EXPERTS : EXPERTS + 2].T
    return gains[None], jnp.stack([q, k, v], axis=1)[None], o[None], small[None, :, :EXPERTS]


def body(images, cotangent, norm_gains, attn_qkv, attn_out, router, expert_in, expert_out, routes):
    section = lax.axis_index("section")
    core = section.astype(jnp.int32).reshape(1)
    on_first = section == 0

    first, second = pack(norm_gains, attn_qkv, attn_out, router)
    mine = jnp.where(on_first, first, second)
    theirs = swap(jnp.where(on_first, second, first))
    own0 = gather_now(jnp.where(on_first, mine, theirs))
    own1 = gather_later(jnp.where(on_first, theirs, mine))

    w1, w2 = expert_in[0], expert_out[0]
    chosen = jnp.pad(routes[0], ((0, 0), (0, 0), (0, SPAN - SEQ), (0, 126)), constant_values=-1)
    chosen = chosen.reshape(2, PAD, 128)
    own0, w1_other, w2_other, chosen_other = lax.optimization_barrier(
        (own0, swap(w1), swap(w2), swap(chosen))
    )
    routed = (chosen, chosen_other)
    weights = (w1, w1_other, w2, w2_other)
    other0 = swap(own0)

    buf_shape = ((FILL, WIDTH), BF)
    wide_shape = ((FILL, 2 * WIDTH), BF)
    tok_b = ((2, SEQ, WIDTH), BF)
    tok_f = ((2, SEQ, WIDTH), F32)

    buf, *saved0 = whole_call(
        first_kernel, "first", [buf_shape] + SAVED, (core, images, *routed), (own0, other0)
    )
    rows0 = exchange(buf)
    y, q0, gp0 = expert_call(
        expert_forward_kernel, "expert_forward", 0, core, [rows0], weights,
        [(FILL, WIDTH), (FILL, HIDDEN), (FILL, HIDDEN)],
    )
    back = exchange(y)
    own1, _ = lax.optimization_barrier((own1, y))
    other1 = swap(own1)
    h0, c0 = saved0[3], saved0[5]
    x1, y_both, buf, *saved1 = whole_call(
        middle_kernel, "middle", [tok_b, ((PAD, 2 * WIDTH), BF), wide_shape] + SAVED,
        (core, back, h0, c0, *routed, cotangent), (own1, other1),
    )
    rows1 = exchange(buf)
    back, q1, df1 = expert_call(
        expert_both_kernel, "expert_both", 1, core, [rows1], weights,
        [(FILL, 2 * WIDTH), (FILL, HIDDEN), (FILL, HIDDEN)],
    )
    g1_1, g2_1 = expert_grads("expert_grads_1", rows1, rows1, 1, q1, df1)
    to_second, to_first = [(0, 1)], [(1, 0)]
    back, g1_1, g2_1 = lax.optimization_barrier((exchange(back), g1_1, g2_1))
    out_keep, out_send, dx1, ga_keep, ga_send, buf, dgv = whole_call(
        turn_kernel, "turn",
        [tok_b, tok_b, ((PAD, WIDTH), F32), GRADS, GRADS, buf_shape, ((PAD, 128), F32)],
        (core, back, *routed, cotangent, x1, *saved1, y_both, c0), (own1, other1),
    )
    dy0 = exchange(buf)
    partial1 = ga_keep + swap(ga_send)
    partial1, dy0 = lax.optimization_barrier((partial1, dy0))
    rows1_sum = lax.psum_scatter(partial1, "row", scatter_dimension=0, tiled=True)
    back, df0 = expert_call(
        expert_backward_kernel, "expert_backward", 0, core,
        [dy0], weights, [(FILL, WIDTH), (FILL, HIDDEN)], (gp0,),
    )
    g1_0, g2_0 = expert_grads("expert_grads_0", rows0, dy0, 0, q0, df0)
    back, g1_0, g2_0, out_got = lax.optimization_barrier(
        (exchange(back), g1_0, g2_0, swap(out_send))
    )
    r1_1 = lax.ppermute(g1_1, "section", to_second)
    r2_1 = lax.ppermute(g2_1, "section", to_second)
    r1_0 = lax.ppermute(g1_0, "section", to_first)
    r2_0 = lax.ppermute(g2_0, "section", to_first)
    dx_keep, dx_send, ga_keep, ga_send = whole_call(
        last_kernel, "last", [tok_f, tok_f, GRADS, GRADS],
        (core, back, *routed, dx1, dgv, images, *saved0), (own0, other0),
    )
    g1_0, dx_keep, rows1_sum = lax.optimization_barrier((g1_0, dx_keep, rows1_sum))
    planes1_sum, place = reduce_x(rows1_sum)
    partial0, planes1_sum = lax.optimization_barrier((ga_keep + swap(ga_send), planes1_sum))
    received0 = spread_out(partial0)
    total1 = reduce_step(planes1_sum, place, 1)
    grad_first, grad_second = pair_sum(
        "sum_experts", core, [(g1_0, r1_0, g1_1, r1_1), (g2_0, r2_0, g2_1, r2_1)], F32, 6
    )
    received0, grad_first, grad_second, dx_got = lax.optimization_barrier(
        (received0, grad_first, grad_second, swap(dx_send))
    )
    total0 = add_up(received0)

    def order(kept, got):
        return jnp.where(on_first, kept, got), jnp.where(on_first, got, kept)

    section_out = jnp.stack(order(out_keep, out_got))[None]
    input_grads = jnp.stack(order(dx_keep, dx_got))[None]
    kept, sent = jnp.where(on_first, total0, total1), jnp.where(on_first, total1, total0)
    gains, qkv, out, rout = unpack(*order(kept, swap(sent)))
    return (section_out, input_grads, gains, qkv, out, rout, grad_first[None], grad_second[None])


def solution(mesh):
    in_specs = (
        P(None, ("row", "col"), None, None),
        P(None, ("row", "col"), None, None),
        P("section", None, ("row", "col")),
        P("section", "col", None, "row"),
        P("section", "row", "col"),
        P("section", ("row", "col"), None),
        P("section", None, ("row", "col")),
        P("section", ("row", "col"), None),
        P("section", None, ("row", "col"), None, None),
    )
    out_specs = (
        P("section", None, ("row", "col"), None, None),
        P("section", None, ("row", "col"), None, None),
        P("section", None, ("row", "col")),
        P("section", "col", None, "row"),
        P("section", "row", "col"),
        P("section", ("row", "col"), None),
        P("section", None, ("row", "col")),
        P("section", ("row", "col"), None),
    )
    return jax.shard_map(body, mesh=mesh, in_specs=in_specs, out_specs=out_specs, check_vma=False)
```

```python
import functools

import jax
import jax.numpy as jnp
from jax import lax
from jax.experimental import pallas as pl
from jax.experimental.pallas import tpu as pltpu
from jax.sharding import PartitionSpec as P

HEAD = 64
WIDTH = 768
SEQ = 50
SPAN = 56
PAD = 2 * SPAN
EXPERTS = 32
SLOTS = 8
ROWS = 4
COLS = 16
CHIPS = ROWS * COLS
PART = WIDTH // COLS
SMALL = WIDTH // CHIPS
FILL = CHIPS * SLOTS
HIDDEN = 1536
STEP = 512
EPSILON = 1e-06
SCALE = float(HEAD) ** (-0.5)
VMEM = 58 * 1024 * 1024
BF = jnp.bfloat16
F32 = jnp.float32


def dot(left, right):
    return jnp.dot(left, right, preferred_element_type=F32)


def dot_tn(left, right):
    return lax.dot_general(left, right, (((0,), (0,)), ((), ())), preferred_element_type=F32)


def dot_nt(left, right):
    return lax.dot_general(left, right, (((1,), (1,)), ((), ())), preferred_element_type=F32)


def iota(shape, axis):
    return lax.broadcasted_iota(jnp.int32, shape, axis)


def hot(flag):
    return jnp.where(flag, 1.0, 0.0)


def normalise(values):
    centred = values - jnp.mean(values, axis=-1, keepdims=True)
    spread = jnp.mean(centred * centred, axis=-1, keepdims=True)
    inverse = lax.rsqrt(spread + EPSILON)
    return centred * inverse, inverse


def normalise_back(grad, unit, inverse):
    return inverse * (
        grad
        - jnp.mean(grad, axis=-1, keepdims=True)
        - unit * jnp.mean(grad * unit, axis=-1, keepdims=True)
    )


def gelu_parts(values):
    bell = jnp.exp(-0.5 * values * values)
    t = 1.0 / (1.0 + (0.3275911 * 0.7071067811865476) * jnp.abs(values))
    poly = 1.061405429 * t - 1.453152027
    poly = poly * t + 1.421413741
    poly = poly * t - 0.284496736
    poly = poly * t + 0.254829592
    tail = (0.5 * t) * poly * bell
    below = jnp.where(values < 0, tail, 1.0 - tail)
    return values * below, below + values * (0.3989422804014327 * bell)


def half_turn(values):
    return pltpu.roll(values, HEAD, 1)


def lane_low(rows):
    return iota((rows, 2 * HEAD), 1) < HEAD


def weight_reader(core, own_ref, other_ref, w_ref, small_ref, sems):
    small_copy = pltpu.make_async_copy(own_ref.at[:, 3 * PART : 3 * PART + 16, :], small_ref, sems.at[6, 0])
    small_copy.start()

    def copy(ref, half, r, b):
        at = (3 * half + b) * 128
        return pltpu.make_async_copy(
            ref.at[r * COLS : (r + 1) * COLS, b * PART : (b + 1) * PART, :],
            w_ref.at[r, :, :, at : at + 128],
            sems.at[3 * half + b, r],
        )

    def start(refs):
        for r in range(ROWS):
            for half in range(2):
                for b in range(3):
                    copy(refs[half], half, r, b).start()

    @pl.when(core == 0)
    def _():
        start((own_ref, other_ref))

    @pl.when(core == 1)
    def _():
        start((other_ref, own_ref))

    def wait():
        for r in range(ROWS):
            for half in range(2):
                for b in range(3):
                    copy(own_ref, half, r, b).wait()

    def read(r, first, last):
        return w_ref[r, :, :, first:last].reshape(WIDTH, last - first)

    return small_copy.wait, wait, read


def small_places():
    shape = (COLS * SMALL, COLS * 16)
    inside = iota(shape, 1)
    place = jnp.bitwise_and(inside, 15)
    wanted = lax.shift_right_logical(inside, 4) * SMALL + place
    return hot((iota(shape, 0) == wanted) & (place < SMALL)).astype(BF)


def unpack_small(small_ref):
    packed = small_ref[...].reshape(ROWS, COLS * 16, 128)
    places = small_places()
    small = jnp.concatenate([dot(places, packed[r]) for r in range(ROWS)], axis=0).astype(BF)
    pick = hot(iota((8, 128), 1) == iota((8, 128), 0) + EXPERTS).astype(BF)
    gains = dot_nt(pick, small)
    return small, gains[0:1], gains[1:2]


def routing(core, section, own_ref, other_ref):
    chosen = jnp.where(core == section, own_ref[core], other_ref[core])
    first = chosen[:, 0:1]
    second = chosen[:, 1:2]
    lane = iota((PAD, 128), 1)
    hot0 = hot(lane == first)
    hot1 = hot(lane == second)
    before = hot(iota((PAD, PAD), 0) > iota((PAD, PAD), 1)).astype(BF)
    earlier = dot(before, (hot0 + hot1).astype(BF))
    place = iota((PAD, FILL), 1)

    def spread(expert, marks):
        slot = jnp.sum(earlier * marks, axis=1, keepdims=True).astype(jnp.int32)
        base = expert * (2 * SLOTS) + slot
        return hot((place == base) | (place == base + SLOTS)).astype(BF)

    return hot0, hot1, spread(first, hot0), spread(second, hot1)


def gates(chance, marks):
    return jnp.sum(chance * marks, axis=1, keepdims=True)


def image_bias():
    query = iota((PAD, PAD), 0)
    key = iota((PAD, PAD), 1)
    first = (query < SPAN) & (key < SEQ)
    second = (query >= SPAN) & (key >= SPAN) & (key < SPAN + SEQ)
    bias = jnp.where(first | second, 0.0, -1e30)
    return jnp.concatenate([bias] * 3, axis=0)


def read_tokens(ref):
    blank = jnp.zeros((SPAN - SEQ, WIDTH), F32)
    return jnp.concatenate([ref[0].astype(F32), blank, ref[1].astype(F32), blank], axis=0)


def write_tokens(ref, values):
    ref[0] = values[:SEQ].astype(ref.dtype)
    ref[1] = values[SPAN : SPAN + SEQ].astype(ref.dtype)


def attention_forward(x, wait, read, gain, m_ref, p_ref, o_ref):
    unit, _ = normalise(x)
    a = (unit * gain).astype(BF)
    low = lane_low(PAD)
    low_b = hot(low).astype(BF)
    high_b = (1.0 - hot(low)).astype(BF)
    bias = image_bias()
    branch = jnp.zeros((PAD, WIDTH), F32)
    wait()
    for r in range(ROWS):
        wide = dot(a, read(r, 0, 512))
        m5 = dot(a, read(r, 640, 768)).astype(BF)
        m = wide.astype(BF)
        m_ref[:, r * 640 : r * 640 + 512] = m
        m_ref[:, r * 640 + 512 : r * 640 + 640] = m5
        q, k, v, qk = m[:, 0:128], m[:, 128:256], m[:, 256:384], m[:, 384:512]
        k2 = half_turn(wide[:, 384:512]).astype(BF)
        qs = jnp.concatenate([q * low_b, q * high_b], axis=0)
        s = jnp.concatenate([dot_nt(qs, k), dot_nt(qk * low_b, k2)], axis=0)
        s = s * SCALE + bias
        e = jnp.exp(s - jnp.max(s, axis=-1, keepdims=True))
        p = (e / jnp.sum(e, axis=-1, keepdims=True)).astype(BF)
        p_ref[r * 3 * PAD : (r + 1) * 3 * PAD, :] = p
        os = dot(p[: 2 * PAD], v)
        o2 = dot(p[2 * PAD :], m5)
        o01 = jnp.where(low, os[:PAD], os[PAD:])
        o2 = jnp.where(low, 0.0, half_turn(o2))
        o = jnp.concatenate([o01, o2], axis=1).astype(BF)
        o_ref[:, r * 256 : (r + 1) * 256] = o
        branch = branch + dot_nt(o, read(r, 512, 768))
    return x + branch


def route_forward(h, small, gain):
    unit, _ = normalise(h)
    b = (unit * gain).astype(BF)
    logits = dot(b, small)
    inside = iota((PAD, 128), 1) < EXPERTS
    logits = jnp.where(inside, logits, -1e30)
    e = jnp.exp(logits - jnp.max(logits, axis=-1, keepdims=True))
    e = jnp.where(inside, e, 0.0)
    return b, e / jnp.sum(e, axis=-1, keepdims=True)


def attention_backward(dh, x, gain, wait, read, m_ref, p_ref, o_ref, take):
    db = dh.astype(BF)
    unit, inverse = normalise(x)
    a = (unit * gain).astype(BF)
    low = lane_low(PAD)
    low_b = hot(low).astype(BF)
    high_b = (1.0 - hot(low)).astype(BF)
    da = jnp.zeros((PAD, WIDTH), F32)
    wait()
    for r in range(ROWS):
        o = o_ref[:, r * 256 : (r + 1) * 256]
        q = m_ref[:, r * 640 : r * 640 + 128]
        k = m_ref[:, r * 640 + 128 : r * 640 + 256]
        v = m_ref[:, r * 640 + 256 : r * 640 + 384]
        qk = m_ref[:, r * 640 + 384 : r * 640 + 512]
        m5 = m_ref[:, r * 640 + 512 : r * 640 + 640]
        k2 = half_turn(qk.astype(F32)).astype(BF)
        q2 = qk * low_b
        qs = jnp.concatenate([q * low_b, q * high_b], axis=0)
        pb = p_ref[r * 3 * PAD : (r + 1) * 3 * PAD, :]
        p = pb.astype(F32)
        do = dot(db, read(r, 512, 768))
        do01 = do[:, 0:128].astype(BF)
        do2 = half_turn(do[:, 128:256]).astype(BF) * low_b
        dos = jnp.concatenate([do01 * low_b, do01 * high_b], axis=0)
        dp = jnp.concatenate([dot_nt(dos, v), dot_nt(do2, m5)], axis=0)
        ds = (p * (dp - jnp.sum(dp * p, axis=-1, keepdims=True))).astype(BF)
        dv = dot_tn(pb[: 2 * PAD], dos)
        dv2 = dot_tn(pb[2 * PAD :], do2)
        dqs = dot(ds[: 2 * PAD], k)
        dq = jnp.where(low, dqs[:PAD], dqs[PAD:]) * SCALE
        dk = dot_tn(ds[: 2 * PAD], qs) * SCALE
        dq2 = dot(ds[2 * PAD :], k2) * SCALE
        dk2 = dot_tn(ds[2 * PAD :], q2) * SCALE
        dqk = jnp.where(low, dq2, half_turn(dk2))
        dm = jnp.concatenate([dq, dk, dv, dqk, dv2], axis=1).astype(BF)
        da = da + dot_nt(dm[:, :512], read(r, 0, 512)) + dot_nt(dm[:, 512:], read(r, 640, 768))
        take(r, a, db, dm)
    dx = dh + normalise_back(da * gain, unit, inverse)
    return dx, a, db, (da * unit).astype(BF)


def projection_grads(r, a, db, dm, o, g_ref):
    gm = dot_tn(a, dm)
    go = dot_tn(db, o)
    blocks = [gm[:, i * 128 : (i + 1) * 128] for i in range(4)]
    blocks += [go[:, :128], gm[:, 512:640] + go[:, 128:256]]
    for i, block in enumerate(blocks):
        at = i % 3 * PART
        g_ref[i // 3, r * COLS : (r + 1) * COLS, at : at + PART, :] = block.astype(BF).reshape(
            COLS, PART, 128
        )


def small_grads(b, dl, terms1, terms2, g_ref):
    lane = iota((PAD, 128), 1)
    gs = dot_tn(b, dl)
    gs = gs + dot_tn(terms1, hot(lane == EXPERTS).astype(BF))
    gs = gs + dot_tn(terms2, hot(lane == EXPERTS + 1).astype(BF))
    gs = gs.astype(BF).reshape(ROWS, COLS * SMALL, 128)
    places = small_places()
    spread = jnp.concatenate([dot_tn(places, gs[r]) for r in range(ROWS)], axis=0).astype(BF)
    spread = spread.reshape(CHIPS, 16, 128)
    g_ref[0, :, 3 * PART :, :] = spread
    g_ref[1, :, 3 * PART :, :] = spread


def layer_backward(dz, dr, marks, dgv, x, h, chance, small, gain1, gain2, wait, read, m_ref, p_ref, o_ref, take):
    _, _, d0, d1 = marks
    dn = dot(d0, dr).astype(BF).astype(F32) + dot(d1, dr).astype(BF).astype(F32)
    dl = (chance * (dgv - jnp.sum(dgv * chance, axis=1, keepdims=True))).astype(BF)
    dn = dn + dot_nt(dl, small)
    unit, inverse = normalise(h)
    dh = dz + normalise_back(dn * gain2, unit, inverse)
    dx, a, db, terms1 = attention_backward(dh, x, gain1, wait, read, m_ref, p_ref, o_ref, take)
    return dx, (a, db, dl, terms1, (dn * unit).astype(BF))


def ship(core, rows, part, g_ref, keep_ref, send_ref, sems):
    here = (slice(0, CHIPS), rows)
    return send([
        (g_ref.at[(1 - core,) + here], send_ref.at[here], sems.at[0, part]),
        (g_ref.at[(core,) + here], keep_ref.at[here], sems.at[1, part]),
    ])


def gate_grads(dz, y_both, marks):
    hot0, hot1 = marks[0], marks[1]
    dg0 = jnp.sum(dz * y_both[:, :WIDTH].astype(F32), axis=1, keepdims=True)
    dg1 = jnp.sum(dz * y_both[:, WIDTH:].astype(F32), axis=1, keepdims=True)
    return dg0 * hot0 + dg1 * hot1


def grad_rows(dz, chance, marks):
    hot0, hot1, d0, d1 = marks
    dy0 = (gates(chance, hot0) * dz).astype(BF)
    dy1 = (gates(chance, hot1) * dz).astype(BF)
    return (dot_tn(d0, dy0) + dot_tn(d1, dy1)).astype(BF)


def combine(h, returned, chance, marks):
    hot0, hot1, d0, d1 = marks
    y0 = dot(d0, returned).astype(BF)
    y1 = dot(d1, returned).astype(BF)
    z = h + gates(chance, hot0) * y0.astype(F32) + gates(chance, hot1) * y1.astype(F32)
    return z, jnp.concatenate([y0, y1], axis=1)


def first_kernel(core_ref, x_ref, routes_ref, routes_other_ref, own_ref, other_ref, buf_ref, m_ref, p_ref, o_ref, h_ref, b_ref, c_ref, w_ref, small_ref, w_sems):
    core = core_ref[0]
    ready, wait, read = weight_reader(core, own_ref, other_ref, w_ref, small_ref, w_sems)
    ready()
    small, gain1, gain2 = unpack_small(small_ref)
    marks = routing(core, 0, routes_ref, routes_other_ref)
    h = attention_forward(read_tokens(x_ref.at[core]), wait, read, gain1, m_ref, p_ref, o_ref)
    b, chance = route_forward(h, small, gain2)
    h_ref[...] = h
    b_ref[...] = b
    c_ref[...] = chance
    buf_ref[...] = dot_tn(marks[2] + marks[3], b).astype(BF)


def middle_kernel(core_ref, back_ref, h0_ref, c0_ref, routes_ref, routes_other_ref, cot_ref, own_ref, other_ref, x_ref, y_ref, buf_ref, m_ref, p_ref, o_ref, h_ref, b_ref, c_ref, w_ref, small_ref, w_sems):
    core = core_ref[0]
    ready, wait, read = weight_reader(core, own_ref, other_ref, w_ref, small_ref, w_sems)
    marks = routing(core, 0, routes_ref, routes_other_ref)
    z, y_both = combine(h0_ref[...], back_ref[...], c0_ref[...], marks)
    write_tokens(x_ref, z)
    y_ref[...] = y_both
    ready()
    small, gain1, gain2 = unpack_small(small_ref)
    marks = routing(core, 1, routes_ref, routes_other_ref)
    x = read_tokens(x_ref)
    h = attention_forward(x, wait, read, gain1, m_ref, p_ref, o_ref)
    b, chance = route_forward(h, small, gain2)
    h_ref[...] = h
    b_ref[...] = b
    c_ref[...] = chance
    buf_ref[:, :WIDTH] = dot_tn(marks[2] + marks[3], b).astype(BF)
    buf_ref[:, WIDTH:] = grad_rows(read_tokens(cot_ref.at[core]), chance, marks)


def turn_kernel(core_ref, back_ref, routes_ref, routes_other_ref, cot_ref, x_ref, m_ref, p_ref, o_ref, h_ref, b_ref, c_ref, y0_ref, c0_ref, own_ref, other_ref, keep_ref, send_ref, dx_ref, gk_ref, gs_ref, buf_ref, dgv_ref, w_ref, small_ref, w_sems, g_ref, sems):
    core = core_ref[0]
    ready, wait, read = weight_reader(core, own_ref, other_ref, w_ref, small_ref, w_sems)
    ready()
    small, gain1, gain2 = unpack_small(small_ref)
    marks = routing(core, 1, routes_ref, routes_other_ref)
    chance = c_ref[...]
    h = h_ref[...]
    z, y_both = combine(h, back_ref[:, :WIDTH], chance, marks)
    x = read_tokens(x_ref)
    on_first = core == 0
    write_tokens(keep_ref, jnp.where(on_first, x, z))
    write_tokens(send_ref, jnp.where(on_first, z, x))
    dz = read_tokens(cot_ref.at[core])
    dgv = gate_grads(dz, y_both, marks)

    copies = []

    def take(r, a, db, dm):
        projection_grads(r, a, db, dm, o_ref[:, r * 256 : (r + 1) * 256], g_ref)
        if r == ROWS - 1:
            copies.extend(ship(core, slice(0, 3 * PART), 0, g_ref, gk_ref, gs_ref, sems))

    dx, terms = layer_backward(dz, back_ref[:, WIDTH:], marks, dgv, x, h, chance, small, gain1, gain2, wait, read, m_ref, p_ref, o_ref, take)
    dx_ref[...] = dx
    small_grads(b_ref[...], *terms[2:], g_ref)
    copies += ship(core, slice(3 * PART, 3 * PART + 16), 1, g_ref, gk_ref, gs_ref, sems)
    dz = dx.astype(BF).astype(F32)
    marks = routing(core, 0, routes_ref, routes_other_ref)
    buf_ref[...] = grad_rows(dz, c0_ref[...], marks)
    dgv_ref[...] = gate_grads(dz, y0_ref[...], marks)
    for copy in copies:
        copy.wait()


def last_kernel(core_ref, back_ref, routes_ref, routes_other_ref, dz_ref, dgv_ref, x_ref, m_ref, p_ref, o_ref, h_ref, b_ref, c_ref, own_ref, other_ref, keep_ref, send_ref, gk_ref, gs_ref, w_ref, small_ref, w_sems, g_ref, sems):
    core = core_ref[0]
    ready, wait, read = weight_reader(core, own_ref, other_ref, w_ref, small_ref, w_sems)
    ready()
    small, gain1, gain2 = unpack_small(small_ref)
    marks = routing(core, 0, routes_ref, routes_other_ref)
    dx1 = dz_ref[...]
    dz = dx1.astype(BF).astype(F32)

    copies = []

    def take(r, a, db, dm):
        projection_grads(r, a, db, dm, o_ref[:, r * 256 : (r + 1) * 256], g_ref)
        if r == ROWS - 1:
            copies.extend(ship(core, slice(0, 3 * PART), 0, g_ref, gk_ref, gs_ref, sems))

    dx, terms = layer_backward(dz, back_ref[...], marks, dgv_ref[...], read_tokens(x_ref.at[core]), h_ref[...], c_ref[...], small, gain1, gain2, wait, read, m_ref, p_ref, o_ref, take)
    small_grads(b_ref[...], *terms[2:], g_ref)
    copies += ship(core, slice(3 * PART, 3 * PART + 16), 1, g_ref, gk_ref, gs_ref, sems)
    on_first = core == 0
    write_tokens(keep_ref, jnp.where(on_first, dx, dx1))
    write_tokens(send_ref, jnp.where(on_first, dx1, dx))
    for copy in copies:
        copy.wait()


def whole_call(kernel, name, outs, args, weights):
    vmem = pl.BlockSpec(memory_space=pltpu.VMEM)
    far = pl.BlockSpec(memory_space=pl.ANY)
    scratch = [
        pltpu.VMEM((ROWS, COLS, PART, WIDTH), BF),
        pltpu.VMEM((CHIPS, 16, 128), BF),
        pltpu.SemaphoreType.DMA((7, ROWS)),
    ]
    if GRADS in outs:
        scratch += [pltpu.VMEM((2,) + GRADS[0], BF), pltpu.SemaphoreType.DMA((2, 2))]
    return pl.pallas_call(
        kernel,
        name=name,
        out_shape=[jax.ShapeDtypeStruct(shape, dtype) for shape, dtype in outs],
        in_specs=[pl.BlockSpec(memory_space=pltpu.SMEM)] + [vmem] * (len(args) - 1) + [far] * len(weights),
        out_specs=[far if out == GRADS else vmem for out in outs],
        scratch_shapes=scratch,
        compiler_params=pltpu.CompilerParams(vmem_limit_bytes=VMEM),
    )(*args, *weights)


SAVED = [
    ((PAD, ROWS * 640), BF),
    ((ROWS * 3 * PAD, PAD), BF),
    ((PAD, ROWS * 256), BF),
    ((PAD, WIDTH), F32),
    ((PAD, WIDTH), BF),
    ((PAD, 128), F32),
]
GRADS = ((CHIPS, 3 * PART + 16, 128), BF)


def fetch(core, section, own_refs, other_refs, places, sems):
    def start(refs):
        for j in range(HIDDEN // STEP):
            here = slice(j * STEP, (j + 1) * STEP)
            pltpu.make_async_copy(refs[0].at[:, here], places[0].at[:, here], sems.at[0, j]).start()
            pltpu.make_async_copy(refs[1].at[here, :], places[1].at[here, :], sems.at[1, j]).start()

    @pl.when(core == section)
    def _():
        start(own_refs)

    @pl.when(core != section)
    def _():
        start(other_refs)


def fetched(own_refs, places, sems, j):
    here = slice(j * STEP, (j + 1) * STEP)
    pltpu.make_async_copy(own_refs[0].at[:, here], places[0].at[:, here], sems.at[0, j]).wait()
    pltpu.make_async_copy(own_refs[1].at[here, :], places[1].at[here, :], sems.at[1, j]).wait()


def add_to(total, j, value):
    total[...] = value if j == 0 else total[...] + value


def send(pairs):
    copies = [pltpu.make_async_copy(*pair) for pair in pairs]
    for copy in copies:
        copy.start()
    return copies


def expert_forward_kernel(section, core_ref, rows_ref, a_ref, b_ref, c_ref, d_ref, y_ref, q_ref, gp_ref, w1, w2, sems, total, q_s, gp_s, out_sems):
    fetch(core_ref[0], section, (a_ref, c_ref), (b_ref, d_ref), (w1, w2), sems)
    copies = []
    for j in range(HIDDEN // STEP):
        fetched((a_ref, c_ref), (w1, w2), sems, j)
        here = slice(j * STEP, (j + 1) * STEP)
        q, gp = gelu_parts(dot(rows_ref[...], w1[:, here]))
        q = q.astype(BF)
        q_s[:, here] = q
        gp_s[:, here] = gp.astype(BF)
        add_to(total, j, dot(q, w2[here, :]))
        copies += send([
            (q_s.at[:, here], q_ref.at[:, here], out_sems.at[0, j]),
            (gp_s.at[:, here], gp_ref.at[:, here], out_sems.at[1, j]),
        ])
    y_ref[...] = total[...].astype(BF)
    for copy in copies:
        copy.wait()


def expert_both_kernel(section, core_ref, rows_ref, a_ref, b_ref, c_ref, d_ref, back_ref, q_ref, df_ref, w1, w2, sems, total, total_back, q_s, df_s, out_sems):
    fetch(core_ref[0], section, (a_ref, c_ref), (b_ref, d_ref), (w1, w2), sems)
    copies = []
    for j in range(HIDDEN // STEP):
        fetched((a_ref, c_ref), (w1, w2), sems, j)
        here = slice(j * STEP, (j + 1) * STEP)
        q, gp = gelu_parts(dot(rows_ref[:, :WIDTH], w1[:, here]))
        q = q.astype(BF)
        q_s[:, here] = q
        df = (dot_nt(rows_ref[:, WIDTH:], w2[here, :]) * gp).astype(BF)
        df_s[:, here] = df
        add_to(total, j, dot(q, w2[here, :]))
        add_to(total_back, j, dot_nt(df, w1[:, here]))
        copies += send([
            (q_s.at[:, here], q_ref.at[:, here], out_sems.at[0, j]),
            (df_s.at[:, here], df_ref.at[:, here], out_sems.at[1, j]),
        ])
    back_ref[:, :WIDTH] = total[...].astype(BF)
    back_ref[:, WIDTH:] = total_back[...].astype(BF)
    for copy in copies:
        copy.wait()


def expert_backward_kernel(section, core_ref, dy_ref, a_ref, b_ref, c_ref, d_ref, gp_far, back_ref, df_ref, w1, w2, sems, total, df_s, out_sems, gp_ref, in_sems):
    fetch(core_ref[0], section, (a_ref, c_ref), (b_ref, d_ref), (w1, w2), sems)
    kept = []
    for j in range(HIDDEN // STEP):
        here = slice(j * STEP, (j + 1) * STEP)
        kept += send([(gp_far.at[:, here], gp_ref.at[:, here], in_sems.at[0, j])])
    copies = []
    for j in range(HIDDEN // STEP):
        here = slice(j * STEP, (j + 1) * STEP)
        fetched((a_ref, c_ref), (w1, w2), sems, j)
        kept[j].wait()
        df = (dot_nt(dy_ref[...], w2[here, :]) * gp_ref[:, here].astype(F32)).astype(BF)
        df_s[:, here] = df
        add_to(total, j, dot_nt(df, w1[:, here]))
        copies += send([(df_s.at[:, here], df_ref.at[:, here], out_sems.at[0, j])])
    back_ref[...] = total[...].astype(BF)
    for copy in copies:
        copy.wait()


def expert_grads_kernel(rows_ref, dy_ref, q_ref, df_ref, g1_ref, g2_ref, turned):
    @pl.when(pl.program_id(0) == 0)
    def _():
        turned[...] = rows_ref[...].T

    g1_ref[...] = dot(turned[...], df_ref[...]).astype(BF)
    g2_ref[...] = dot_tn(q_ref[...], dy_ref[...]).astype(BF)


def expert_grads(name, rows, dy, dy_at, q, df):
    return pl.pallas_call(
        expert_grads_kernel,
        name=name,
        out_shape=[
            jax.ShapeDtypeStruct((WIDTH, HIDDEN), BF),
            jax.ShapeDtypeStruct((HIDDEN, WIDTH), BF),
        ],
        grid=(HIDDEN // STEP,),
        in_specs=[
            pl.BlockSpec((FILL, WIDTH), lambda i: (0, 0)),
            pl.BlockSpec((FILL, WIDTH), lambda i: (0, dy_at)),
            pl.BlockSpec((FILL, STEP), lambda i: (0, i)),
            pl.BlockSpec((FILL, STEP), lambda i: (0, i)),
        ],
        out_specs=[
            pl.BlockSpec((WIDTH, STEP), lambda i: (0, i)),
            pl.BlockSpec((STEP, WIDTH), lambda i: (i, 0)),
        ],
        scratch_shapes=[pltpu.VMEM((WIDTH, FILL), BF)],
        compiler_params=pltpu.CompilerParams(vmem_limit_bytes=VMEM),
    )(rows, dy, q, df)


def expert_call(kernel, name, section, core, arrays, weights, outs, kept=()):
    vmem = pl.BlockSpec(memory_space=pltpu.VMEM)
    far = pl.BlockSpec(memory_space=pl.ANY)
    rows_f = pltpu.VMEM((FILL, WIDTH), F32)
    hid = pltpu.VMEM((FILL, HIDDEN), BF)
    first, second = pltpu.VMEM((WIDTH, HIDDEN), BF), pltpu.VMEM((HIDDEN, WIDTH), BF)
    sems = pltpu.SemaphoreType.DMA((2, HIDDEN // STEP))
    scratch = {
        "expert_forward": [first, second, sems, rows_f, hid, hid, sems],
        "expert_both": [first, second, sems, rows_f, rows_f, hid, hid, sems],
        "expert_backward": [first, second, sems, rows_f, hid, sems, hid, sems],
    }[name]
    return pl.pallas_call(
        functools.partial(kernel, section),
        name=name,
        out_shape=[jax.ShapeDtypeStruct(shape, BF) for shape in outs],
        in_specs=[pl.BlockSpec(memory_space=pltpu.SMEM)] + [vmem] * len(arrays) + [far] * (4 + len(kept)),
        out_specs=[vmem] + [far] * (len(outs) - 1),
        scratch_shapes=scratch,
        compiler_params=pltpu.CompilerParams(vmem_limit_bytes=VMEM),
    )(core, *arrays, *weights, *kept)


def pair_sum_kernel(count, core_ref, *refs):
    for i in range(count):
        a, b, c, d = refs[4 * i : 4 * i + 4]
        out = refs[4 * count + i]

        @pl.when(core_ref[0] == 0)
        def _(a=a, b=b, out=out):
            out[...] = (a[...].astype(F32) + b[...].astype(F32)).astype(out.dtype)

        @pl.when(core_ref[0] == 1)
        def _(c=c, d=d, out=out):
            out[...] = (c[...].astype(F32) + d[...].astype(F32)).astype(out.dtype)


def pair_sum(name, core, groups, dtype, steps):
    def spec(shape, section):
        block = (shape[0] // steps,) + shape[1:]

        def index(i, core_ref):
            here = i if section is None else jnp.where(core_ref[0] == section, i, 0)
            return (here,) + (0,) * (len(shape) - 1)

        return pl.BlockSpec(block, index)

    return pl.pallas_call(
        functools.partial(pair_sum_kernel, len(groups)),
        name=name,
        out_shape=[jax.ShapeDtypeStruct(group[0].shape, dtype) for group in groups],
        grid_spec=pltpu.PrefetchScalarGridSpec(
            num_scalar_prefetch=1,
            grid=(steps,),
            in_specs=[spec(group[0].shape, section) for group in groups for section in (0, 0, 1, 1)],
            out_specs=[spec(group[0].shape, None) for group in groups],
        ),
        compiler_params=pltpu.CompilerParams(vmem_limit_bytes=VMEM),
    )(core, *[array for group in groups for array in group])


SWAP = [(0, 1), (1, 0)]
CHIP = ("row", "col")


def swap(values):
    return lax.ppermute(values, "section", SWAP)


def exchange(rows):
    wide = rows.shape[1]
    out = lax.all_to_all(
        rows.reshape(CHIPS, SLOTS, wide), CHIP, split_axis=0, concat_axis=0, tiled=True
    )
    return out.reshape(FILL, wide)


def gather_now(chunk):
    copies = jnp.broadcast_to(chunk[None], (CHIPS,) + chunk.shape)
    return lax.all_to_all(copies, CHIP, split_axis=0, concat_axis=0, tiled=True)


def gather_later(chunk):
    return lax.all_gather(chunk, CHIP, axis=0)


def spread_out(partial):
    return lax.all_to_all(partial, CHIP, split_axis=0, concat_axis=0, tiled=True)


def reduce_step(chunks, mine, stride):
    side = 4
    total = lax.dynamic_index_in_dim(chunks, mine, 0, keepdims=False).astype(F32)
    for turn in range(1, side):
        pairs = []
        for at in range(COLS):
            own = at // stride % side
            pairs.append((at, at + ((own + turn) % side - own) * stride))
        chunk = lax.dynamic_index_in_dim(chunks, (mine + turn) % side, 0, keepdims=False)
        total = total + lax.ppermute(chunk, "col", pairs).astype(F32)
    return total


def reduce_x(values):
    place = lax.axis_index("col")
    chunks = values.reshape((4, 4) + values.shape[1:])
    return reduce_step(chunks, place // 4, 4).astype(BF), place % 4


def add_up(received):
    return jnp.sum(received.astype(F32), axis=0)


def pack(norm_gains, attn_qkv, attn_out, router):
    q, k, v = attn_qkv[0, :, 0], attn_qkv[0, :, 1], attn_qkv[0, :, 2]
    o = attn_out[0].T
    small = jnp.concatenate([router[0], norm_gains[0].T], axis=1)
    small = jnp.pad(small, ((0, 16 - SMALL), (0, 128 - EXPERTS - 2)))
    lo, hi = slice(0, 128), slice(128, 192)
    first = jnp.concatenate([q[:, lo], k[:, lo], v[:, lo], small], axis=0)
    mixed = jnp.concatenate([q[:, hi], k[:, hi]], axis=1)
    last = jnp.concatenate([v[:, hi], o[:, hi]], axis=1)
    second = jnp.concatenate([mixed, o[:, lo], last, small], axis=0)
    return first, second


def unpack(first, second):
    b = [half[i * PART : (i + 1) * PART] for half in (first, second) for i in range(3)]
    q = jnp.concatenate([b[0], b[3][:, :HEAD]], axis=1)
    k = jnp.concatenate([b[1], b[3][:, HEAD:]], axis=1)
    v = jnp.concatenate([b[2], b[5][:, :HEAD]], axis=1)
    o = jnp.concatenate([b[4], b[5][:, HEAD:]], axis=1).T
    small = first[3 * PART : 3 * PART + SMALL]
    gains = small[:, EXPERTS : EXPERTS + 2].T
    return gains[None], jnp.stack([q, k, v], axis=1)[None], o[None], small[None, :, :EXPERTS]


def body(images, cotangent, norm_gains, attn_qkv, attn_out, router, expert_in, expert_out, routes):
    section = lax.axis_index("section")
    core = section.astype(jnp.int32).reshape(1)
    on_first = section == 0

    first, second = pack(norm_gains, attn_qkv, attn_out, router)
    mine = jnp.where(on_first, first, second)
    theirs = swap(jnp.where(on_first, second, first))
    own0 = gather_now(jnp.where(on_first, mine, theirs))
    own1 = gather_later(jnp.where(on_first, theirs, mine))

    w1, w2 = expert_in[0], expert_out[0]
    chosen = jnp.pad(routes[0], ((0, 0), (0, 0), (0, SPAN - SEQ), (0, 126)), constant_values=-1)
    chosen = chosen.reshape(2, PAD, 128)
    own0, w1_other, w2_other, chosen_other = lax.optimization_barrier(
        (own0, swap(w1), swap(w2), swap(chosen))
    )
    routed = (chosen, chosen_other)
    weights = (w1, w1_other, w2, w2_other)
    other0 = swap(own0)

    buf_shape = ((FILL, WIDTH), BF)
    wide_shape = ((FILL, 2 * WIDTH), BF)
    tok_b = ((2, SEQ, WIDTH), BF)
    tok_f = ((2, SEQ, WIDTH), F32)

    buf, *saved0 = whole_call(
        first_kernel, "first", [buf_shape] + SAVED, (core, images, *routed), (own0, other0)
    )
    rows0 = exchange(buf)
    y, q0, gp0 = expert_call(
        expert_forward_kernel, "expert_forward", 0, core, [rows0], weights,
        [(FILL, WIDTH), (FILL, HIDDEN), (FILL, HIDDEN)],
    )
    back = exchange(y)
    own1, _ = lax.optimization_barrier((own1, y))
    other1 = swap(own1)
    h0, c0 = saved0[3], saved0[5]
    x1, y_both, buf, *saved1 = whole_call(
        middle_kernel, "middle", [tok_b, ((PAD, 2 * WIDTH), BF), wide_shape] + SAVED,
        (core, back, h0, c0, *routed, cotangent), (own1, other1),
    )
    rows1 = exchange(buf)
    back, q1, df1 = expert_call(
        expert_both_kernel, "expert_both", 1, core, [rows1], weights,
        [(FILL, 2 * WIDTH), (FILL, HIDDEN), (FILL, HIDDEN)],
    )
    g1_1, g2_1 = expert_grads("expert_grads_1", rows1, rows1, 1, q1, df1)
    to_second, to_first = [(0, 1)], [(1, 0)]
    back, g1_1, g2_1 = lax.optimization_barrier((exchange(back), g1_1, g2_1))
    out_keep, out_send, dx1, ga_keep, ga_send, buf, dgv = whole_call(
        turn_kernel, "turn",
        [tok_b, tok_b, ((PAD, WIDTH), F32), GRADS, GRADS, buf_shape, ((PAD, 128), F32)],
        (core, back, *routed, cotangent, x1, *saved1, y_both, c0), (own1, other1),
    )
    dy0 = exchange(buf)
    partial1 = ga_keep + swap(ga_send)
    partial1, dy0 = lax.optimization_barrier((partial1, dy0))
    rows1_sum = lax.psum_scatter(partial1, "row", scatter_dimension=0, tiled=True)
    back, df0 = expert_call(
        expert_backward_kernel, "expert_backward", 0, core,
        [dy0], weights, [(FILL, WIDTH), (FILL, HIDDEN)], (gp0,),
    )
    g1_0, g2_0 = expert_grads("expert_grads_0", rows0, dy0, 0, q0, df0)
    back, g1_0, g2_0, out_got = lax.optimization_barrier(
        (exchange(back), g1_0, g2_0, swap(out_send))
    )
    r1_1 = lax.ppermute(g1_1, "section", to_second)
    r2_1 = lax.ppermute(g2_1, "section", to_second)
    r1_0 = lax.ppermute(g1_0, "section", to_first)
    r2_0 = lax.ppermute(g2_0, "section", to_first)
    dx_keep, dx_send, ga_keep, ga_send = whole_call(
        last_kernel, "last", [tok_f, tok_f, GRADS, GRADS],
        (core, back, *routed, dx1, dgv, images, *saved0), (own0, other0),
    )
    g1_0, dx_keep, rows1_sum = lax.optimization_barrier((g1_0, dx_keep, rows1_sum))
    planes1_sum, place = reduce_x(rows1_sum)
    partial0, planes1_sum = lax.optimization_barrier((ga_keep + swap(ga_send), planes1_sum))
    received0 = spread_out(partial0)
    total1 = reduce_step(planes1_sum, place, 1)
    grad_first, grad_second = pair_sum(
        "sum_experts", core, [(g1_0, r1_0, g1_1, r1_1), (g2_0, r2_0, g2_1, r2_1)], F32, 6
    )
    received0, grad_first, grad_second, dx_got = lax.optimization_barrier(
        (received0, grad_first, grad_second, swap(dx_send))
    )
    total0 = add_up(received0)

    def order(kept, got):
        return jnp.where(on_first, kept, got), jnp.where(on_first, got, kept)

    section_out = jnp.stack(order(out_keep, out_got))[None]
    input_grads = jnp.stack(order(dx_keep, dx_got))[None]
    kept, sent = jnp.where(on_first, total0, total1), jnp.where(on_first, total1, total0)
    gains, qkv, out, rout = unpack(*order(kept, swap(sent)))
    return (section_out, input_grads, gains, qkv, out, rout, grad_first[None], grad_second[None])


def solution(mesh):
    in_specs = (
        P(None, ("row", "col"), None, None),
        P(None, ("row", "col"), None, None),
        P("section", None, ("row", "col")),
        P("section", "col", None, "row"),
        P("section", "row", "col"),
        P("section", ("row", "col"), None),
        P("section", None, ("row", "col")),
        P("section", ("row", "col"), None),
        P("section", None, ("row", "col"), None, None),
    )
    out_specs = (
        P("section", None, ("row", "col"), None, None),
        P("section", None, ("row", "col"), None, None),
        P("section", None, ("row", "col")),
        P("section", "col", None, "row"),
        P("section", "row", "col"),
        P("section", ("row", "col"), None),
        P("section", None, ("row", "col")),
        P("section", ("row", "col"), None),
    )
    return jax.shard_map(body, mesh=mesh, in_specs=in_specs, out_specs=out_specs, check_vma=False)
```
